512 devices in a mesh: section: 32 (over x_hi, z), dp: 16 (over y, x_lo, core).
Axes of the slice: x: 4 (x_hi: 2, x_lo: 2; x = x_hi * 2 + x_lo), y: 4, z: 16, core: 2. Of those that a mesh axis runs over, the one named last changes fastest.
Arguments:
- stored_inputs: bfloat16 [32, 16, 33, 8, 8192], P('section', 'dp')
- slot_ids: int32 [32, 16, 33], P('section', 'dp'), may hold values from 0 to 32, as said below
- incoming: bfloat16 [32, 16, 8, 8192], P('section', 'dp'), may hold values from -6 to 6
- delta_exp: int32 [32, 16, 16, 8, 64], P('section', 'dp'), may hold values from -7 to -4
- grad_exp: int32 [32, 16, 15, 8, 64], P('section', 'dp'), may hold values from -7 to -4
- norm_gain: float32 [32, 8192], P('section'), may hold values from 0.5 to 1.5
- down_weight: bfloat16 [32, 8192, 64], P('section', 'dp'), may hold values from -0.0625 to 0.0625
- up_weight: bfloat16 [32, 64, 8192], P('section', None, 'dp'), may hold values from -0.09375 to 0.09375
Outputs:
- grad_down: bfloat16 [32, 8192, 64], P('section', 'dp')
- grad_up: bfloat16 [32, 64, 8192], P('section', None, 'dp')
- next_delta: bfloat16 [32, 16, 8, 8192], P('section', 'dp')
The draws below stay inside these ranges and needn't reach their ends.
Inputs may be any that keep to these rules, and one draw needn't show every extreme that they name: Each row slot_ids[s, d, :] holds every slot number once.
All inputs are finite; a program needn't handle non-finite values.
Results may differ from the reference program's by a relative error of at most 0.025.
Values may be sent and summed in bfloat16 or wider, within the bound.
A program may use at most 64 MiB of HBM per device.

```python
import jax
import jax.numpy as jnp
from jax import lax

D = 8192
R = 64
SEQ = 8
K = 16
SLOTS = 33
BLOCKS = 64
SECTIONS = 32
REPLICAS = 16


def shared_slots(key):
    slot_key = jax.random.fold_in(key, 11)
    scores = jax.random.randint(slot_key, (SECTIONS, REPLICAS, SLOTS), 0, 1 << 20)
    scores = scores * SLOTS + jnp.arange(SLOTS, dtype=jnp.int32)
    return jnp.argsort(scores, axis=-1, stable=True).astype(jnp.int32)


def draw_stored_inputs(key, part):
    slot_order = shared_slots(key)
    key = jax.random.fold_in(key, 5)
    chain_key, noise_key, plant_key = jax.random.split(key, 3)
    chains = jax.random.normal(chain_key, (SECTIONS + K, REPLICAS, SEQ, D), jnp.float32)
    noise = jax.random.normal(noise_key, (SECTIONS, REPLICAS, SLOTS, SEQ, D), jnp.float32)
    planted = jax.random.randint(plant_key, (SECTIONS, REPLICAS, SLOTS, SEQ, 1), 0, 8) == 0
    column = jnp.argsort(slot_order, axis=-1).astype(jnp.int32)
    section_index = jnp.arange(SECTIONS, dtype=jnp.int32)[:, None, None]
    chain_index = jnp.clip(section_index - column + K, 0, SECTIONS + K - 1)
    replica_index = jnp.arange(REPLICAS, dtype=jnp.int32)[None, :, None]
    base_rows = chains[chain_index, replica_index]
    in_chain = (column <= K)[:, :, :, None, None]
    small = jnp.where(planted, jnp.float32(1.5), jnp.float32(0.05))
    values = jnp.where(in_chain, base_rows + small * noise, noise)
    return values.astype(jnp.bfloat16)


def draw_slot_ids(key, part):
    return shared_slots(key)


def with_ends(entries, rng, smallest, largest):
    spot = [jax.random.randint(jax.random.fold_in(rng, axis), (), 0, length) for axis, length in enumerate(entries.shape)]
    main_axis = entries.shape.index(max(entries.shape))
    neighbour = spot[:main_axis] + [(spot[main_axis] + 1) % entries.shape[main_axis]] + spot[main_axis + 1:]
    return entries.at[tuple(spot)].set(smallest).at[tuple(neighbour)].set(largest)


def block_scale(own_key, dims, cuts, low, largest):
    def one(position, parts):
        heights = jax.random.uniform(jax.random.fold_in(jax.random.fold_in(own_key, 6), position), (parts,), jnp.float32, low / len(cuts), largest / len(cuts))
        return jnp.repeat(jnp.exp(heights), dims[position] // parts).reshape((-1,) + (1,) * (len(dims) - position - 1))

    loudness = one(*cuts[0])
    for cut in cuts[1:]:
        loudness = loudness * one(*cut)
    return loudness


def centred(rng, shape, width, limit, cuts=(), kind=jnp.bfloat16):
    factor_of = block_scale(rng, shape, cuts, -0.22, 0.18) if cuts else 1.0
    values = jax.random.normal(rng, shape, jnp.float32) * width * factor_of
    return jnp.minimum(jnp.maximum(values, -limit), limit).astype(kind)


def setup_inputs(seed: int = 0) -> dict:
    arg_keys = jax.random.split(jax.random.key(seed), 9)
    return {
        "stored_inputs": draw_stored_inputs(jax.random.fold_in(arg_keys[8], 71), 0),
        "slot_ids": draw_slot_ids(jax.random.fold_in(arg_keys[8], 71), 0),
        "incoming": centred(arg_keys[2], (SECTIONS, REPLICAS, SEQ, D), 1.0, 6.0, ((0, 32), (1, 16))),
        "delta_exp": with_ends(jax.random.randint(arg_keys[3], (SECTIONS, REPLICAS, K, SEQ, BLOCKS), -7, -3), jax.random.fold_in(arg_keys[3], 1), -7, (-3) - 1).astype(jnp.int32),
        "grad_exp": with_ends(jax.random.randint(arg_keys[4], (SECTIONS, REPLICAS, K - 1, SEQ, BLOCKS), -7, -3), jax.random.fold_in(arg_keys[4], 1), -7, (-3) - 1).astype(jnp.int32),
        "norm_gain": jnp.clip(1.0 + 0.1 * jax.random.normal(arg_keys[5], (SECTIONS, D), jnp.float32), 0.5, 1.5),
        "down_weight": centred(arg_keys[6], (SECTIONS, D, R), D ** -0.5, 0.0625, ((0, 32), (1, 16))),
        "up_weight": centred(arg_keys[7], (SECTIONS, R, D), (0.05 / R ** 0.5), 0.09375, ((0, 32), (2, 16))),
    }


EPSILON = 1e-05
LOWEST = -7
HIGHEST = -4

def powers(exponent):
    running = jnp.zeros(exponent.shape, jnp.float32)
    for degree in range(LOWEST, HIGHEST + 1):
        running = running + jnp.where(exponent == degree, jnp.float32(2.0 ** degree), jnp.float32(0.0))
    return running

def quantize(values, exponent):
    scales = powers(exponent)[..., None]
    blocked = values.reshape(values.shape[:-1] + (exponent.shape[-1], 128))
    levels = jnp.clip(blocked / scales, -127.0, 127.0).astype(jnp.bfloat16)
    levels = lax.optimization_barrier(levels)
    restored = levels.astype(jnp.float32) * scales
    return restored.reshape(values.shape).astype(jnp.bfloat16)

def adapter(inputs, norm_gain, down_float, up_float):
    widened = inputs.astype(jnp.float32)
    inverse = lax.rsqrt(lax.optimization_barrier(jnp.mean(widened * widened, axis=-1, keepdims=True)) + EPSILON)
    normed = (widened * inverse * norm_gain[:, None, :]).astype(jnp.bfloat16)
    before = jnp.einsum('srd,sdk->srk', normed.astype(jnp.float32), down_float)
    hidden = jax.nn.silu(before).astype(jnp.bfloat16)
    output = widened + jnp.einsum('srk,skd->srd', hidden.astype(jnp.float32), up_float)
    return (widened, inverse, normed, before, hidden, output)

def reference(stored_inputs, slot_ids, incoming, delta_exp, grad_exp, norm_gain, down_weight, up_weight):
    row_count = REPLICAS * SEQ
    down_float = down_weight.astype(jnp.float32)
    up_float = up_weight.astype(jnp.float32)
    last_section = (jnp.arange(SECTIONS) == SECTIONS - 1)[:, None, None]
    zero_rows = jnp.zeros((1, row_count, D), jnp.bfloat16)

    def flatten(array):
        return array.reshape(SECTIONS, row_count, array.shape[-1])

    def take_slot(column):
        chosen = jnp.take_along_axis(stored_inputs, slot_ids[:, :, column][:, :, None, None, None], axis=2)
        return flatten(chosen[:, :, 0])
    sent_delta = zero_rows
    returned = zero_rows
    normed_list = []
    slope_list = []
    hidden_list = []
    cotangent_list = []
    for tick_index in range(K):
        stored_row = take_slot(tick_index)
        if tick_index == 0:
            inputs = stored_row
        else:
            arrived = jnp.concatenate([zero_rows, sent_delta[:-1]], axis=0)
            inputs = (stored_row.astype(jnp.float32) + arrived.astype(jnp.float32)).astype(jnp.bfloat16)
        widened, inverse, normed, before, hidden, output = adapter(inputs, norm_gain, down_float, up_float)
        copies = jnp.concatenate([take_slot(tick_index + 1)[1:], stored_row[-1:]], axis=0)
        distance = output - copies.astype(jnp.float32)
        sent_delta = quantize(distance, flatten(delta_exp[:, :, tick_index]))
        if tick_index == 0:
            arrived_grad = flatten(incoming)
        else:
            arrived_grad = jnp.concatenate([returned[1:], zero_rows], axis=0)
        cotangent = jnp.where(last_section, distance.astype(jnp.bfloat16), arrived_grad)
        back_inputs = jnp.where(last_section, inputs, take_slot(K + 1 + tick_index))
        back_widened, back_inverse, back_normed, back_before, back_hidden, recomputed = adapter(back_inputs, norm_gain, down_float, up_float)
        slope_grad = jnp.einsum('srd,skd->srk', cotangent.astype(jnp.float32), up_float)
        gate_value = jax.nn.sigmoid(back_before)
        slope_grad = (slope_grad * gate_value * (1.0 + back_before * (1.0 - gate_value))).astype(jnp.bfloat16)
        normed_list.append(back_normed)
        slope_list.append(slope_grad)
        hidden_list.append(back_hidden)
        cotangent_list.append(cotangent)
        if tick_index < K - 1:
            through = jnp.einsum('srk,sdk->srd', slope_grad.astype(jnp.float32), down_float) * norm_gain[:, None, :]
            inner_mean = lax.optimization_barrier(jnp.mean(through * back_widened, axis=-1, keepdims=True))
            result = cotangent.astype(jnp.float32) + back_inverse * through - back_widened * back_inverse ** 3 * inner_mean
            returned = quantize(result, flatten(grad_exp[:, :, tick_index]))
    next_delta = sent_delta.reshape(SECTIONS, REPLICAS, SEQ, D)
    normed_all = jnp.stack(normed_list).reshape(K, SECTIONS, REPLICAS, SEQ, D)
    slope_all = jnp.stack(slope_list).reshape(K, SECTIONS, REPLICAS, SEQ, R)
    hidden_all = jnp.stack(hidden_list).reshape(K, SECTIONS, REPLICAS, SEQ, R)
    cotangent_all = jnp.stack(cotangent_list).reshape(K, SECTIONS, REPLICAS, SEQ, D)
    total_down = jnp.zeros((SECTIONS, D, R), jnp.float32)
    total_up = jnp.zeros((SECTIONS, R, D), jnp.float32)
    for replica in range(REPLICAS):
        replica_term = jnp.einsum('tsqd,tsqk->sdk', normed_all[:, :, replica].astype(jnp.float32), slope_all[:, :, replica].astype(jnp.float32)).astype(jnp.bfloat16)
        replica_term = lax.optimization_barrier(replica_term)
        total_down = total_down + replica_term.astype(jnp.float32)
        replica_term = jnp.einsum('tsqk,tsqd->skd', hidden_all[:, :, replica].astype(jnp.float32), cotangent_all[:, :, replica].astype(jnp.float32)).astype(jnp.bfloat16)
        replica_term = lax.optimization_barrier(replica_term)
        total_up = total_up + replica_term.astype(jnp.float32)
    factor = 1.0 / (K * SEQ)
    grad_down = (total_down * factor).astype(jnp.bfloat16)
    grad_up = (total_up * factor).astype(jnp.bfloat16)
    return (grad_down, grad_up, next_delta)
```

```python
import functools

import jax
import jax.numpy as jnp
from jax import lax
from jax.experimental import pallas as pl
from jax.experimental.pallas import tpu as pltpu
from jax.sharding import PartitionSpec as P

EPSILON = 1e-05
PARTS = 16
FOLD = 4
CHUNKS = 4
LANES = 512
ROWS = 8
RANK = 64
SCALE = 1024.0
NT = (((1,), (1,)), ((), ()))
TN = (((0,), (0,)), ((), ()))
NN = (((1,), (0,)), ((), ()))


def dot(a, b, dims):
    return lax.dot_general(a, b, dims, preferred_element_type=jnp.float32)


def bounds(exponent):
    return jnp.where(
        exponent == -7,
        127.0 * 2.0**-7,
        jnp.where(exponent == -6, 127.0 * 2.0**-6, jnp.where(exponent == -5, 127.0 * 2.0**-5, 127.0 * 2.0**-4)),
    ).astype(jnp.float32)


def spread(table, c):
    per = LANES // 128
    groups = []
    for q in range(FOLD):
        first = q * CHUNKS * per + c * per
        groups.append(
            jnp.concatenate(
                [jnp.broadcast_to(table[:, b : b + 1], (ROWS, 128)) for b in range(first, first + per)], axis=1
            )
        )
    return jnp.concatenate(groups, axis=0)


def clip_to(values, bound):
    return jnp.minimum(jnp.maximum(values, -bound), bound)


def fold_rows(ref, index, c):
    width = CHUNKS * LANES
    parts = []
    for q in range(FOLD):
        lanes = pl.ds(q * width + c * LANES, LANES)
        part = ref[:, lanes] if index is None else ref[index, :, lanes]
        parts.append(part.astype(jnp.float32))
    return jnp.concatenate(parts, axis=0)


def low_half():
    return lax.broadcasted_iota(jnp.int32, (ROWS, 128), 1) < RANK


def gather_groups(product):
    low = low_half()
    first = jnp.where(low, product[0:8, 0:128], product[8:16, 0:128])
    second = jnp.where(low, product[16:24, 128:256], product[24:32, 128:256])
    half = first + second
    return half + pltpu.roll(half, RANK, 1)


def scatter_groups(values):
    low = low_half()
    zero = jnp.zeros_like(values)
    left = jnp.where(low, values, zero)
    right = jnp.where(low, zero, values)
    first = jnp.concatenate([left, right, zero, zero], axis=0)
    second = jnp.concatenate([zero, zero, left, right], axis=0)
    return jnp.concatenate([first, second], axis=1).astype(jnp.bfloat16)


def lane_total(values):
    return jnp.broadcast_to(jnp.sum(values, axis=1, keepdims=True), (ROWS, 128))


def squares(x):
    total = jnp.zeros((ROWS, 128), jnp.float32)
    for q in range(FOLD):
        for i in range(LANES // 128):
            piece = x[q * ROWS : (q + 1) * ROWS, i * 128 : (i + 1) * 128]
            total = total + piece * piece
    return total


def kernel(
    ticks,
    sections,
    slots,
    stored_hbm,
    incoming,
    delta_exp,
    grad_exp,
    gain,
    down,
    up,
    down_out,
    up_out,
    delta_out,
    stored,
    weights,
    forward_in,
    forward_out,
    backward_in,
    backward_out,
    shares_out,
    shares_in,
    exps_in,
    copy_out,
    copy_in,
    x_now,
    back_now,
    stats,
    totals,
    stored_sem,
    weight_send,
    weight_recv,
    forward_send,
    forward_recv,
    backward_send,
    backward_recv,
    share_send,
    share_recv,
    side_send,
    side_recv,
):
    section = lax.axis_index("section")
    me = lax.axis_index("dp")
    is_first = section == 0
    is_last = section == sections - 1
    features = gain.shape[1]

    load_stored = pltpu.make_async_copy(stored_hbm, stored, stored_sem)
    load_stored.start()

    barrier = pltpu.get_barrier_semaphore()

    def peer(offset):
        return lax.rem(me + offset, PARTS)

    for offset in range(1, PARTS):
        pl.semaphore_signal(barrier, inc=1, device_id={"dp": peer(offset)})

    @pl.when(jnp.logical_not(is_first))
    def _():
        pl.semaphore_signal(barrier, inc=1, device_id={"section": section - 1})

    @pl.when(jnp.logical_not(is_last))
    def _():
        pl.semaphore_signal(barrier, inc=1, device_id={"section": section + 1})

    group = me // CHUNKS
    chunk = lax.rem(me, CHUNKS)
    group_rows = pl.ds(pl.multiple_of(group * RANK, RANK), RANK)
    own_lanes = pl.ds(pl.multiple_of(me * LANES, LANES), LANES)
    own_gain = gain[:, own_lanes]
    weights[0, chunk, group_rows, :] = (down[...].astype(jnp.float32) * (own_gain * (1.0 / SCALE))).astype(jnp.bfloat16)
    weights[1, chunk, group_rows, :] = up[...]
    totals[...] = jnp.zeros_like(totals)

    ends = jnp.where(is_first, 1, 0) + jnp.where(is_last, 1, 0)
    pl.semaphore_wait(barrier, PARTS + 1 - ends)

    def weight_copy(which, offset):
        block = weights.at[which, chunk, group_rows, :]
        return pltpu.make_async_remote_copy(
            src_ref=block,
            dst_ref=block,
            send_sem=weight_send.at[which, offset],
            recv_sem=weight_recv.at[which, me],
            device_id={"dp": peer(offset)},
        )

    def weight_arrival(which, offset):
        source = peer(offset)
        rows = pl.ds(pl.multiple_of((source // CHUNKS) * RANK, RANK), RANK)
        block = weights.at[which, lax.rem(source, CHUNKS), rows, :]
        return pltpu.make_async_remote_copy(
            src_ref=block,
            dst_ref=block,
            send_sem=weight_send.at[which, offset],
            recv_sem=weight_recv.at[which, source],
            device_id={"dp": source},
        )

    for which in range(2):
        for offset in range(1, PARTS):
            weight_copy(which, offset).start()

    exps_copy = pltpu.make_async_remote_copy(
        src_ref=delta_exp,
        dst_ref=exps_in,
        send_sem=side_send.at[0],
        recv_sem=side_recv.at[0],
        device_id={"section": section + 1},
    )

    @pl.when(jnp.logical_not(is_last))
    def _():
        exps_copy.start()

    load_stored.wait()

    copy_copy = pltpu.make_async_remote_copy(
        src_ref=copy_out,
        dst_ref=copy_in,
        send_sem=side_send.at[1],
        recv_sem=side_recv.at[1],
        device_id={"section": section - 1},
    )

    @pl.when(jnp.logical_not(is_first))
    def _():
        for c in range(CHUNKS):
            copy_out[c] = fold_rows(stored, slots[ticks], c).astype(jnp.bfloat16)
        copy_copy.start()

    @pl.when(jnp.logical_not(is_last))
    def _():
        for c in range(CHUNKS):
            backward_in[0, c] = fold_rows(incoming, None, c).astype(jnp.bfloat16)

    for offset in range(1, PARTS):
        weight_arrival(0, offset).wait_recv()

    def row_stats(product, total):
        inverse = lax.rsqrt(lane_total(total) * (1.0 / features) + EPSILON)
        before = gather_groups(product) * (inverse * SCALE)
        gate = 1.0 / (1.0 + jnp.exp(-before))
        return inverse, before, gate

    def keep_stats(inverse, before, gate):
        stats[0] = inverse
        stats[1] = before
        stats[2] = gate * (1.0 + before * (1.0 - gate))
        stats[3] = before * gate

    def prepare(tick):
        product = jnp.zeros((FOLD * ROWS, FOLD * RANK), jnp.float32)
        total = jnp.zeros((ROWS, 128), jnp.float32)
        for c in range(CHUNKS):
            rows = fold_rows(stored, slots[ticks + 1 + tick], c)
            narrow = rows.astype(jnp.bfloat16)
            back_now[c] = narrow
            product = product + dot(narrow, weights[0, c], NT)
            total = total + squares(rows)
        keep_stats(*row_stats(product, total))

    @pl.when(jnp.logical_not(is_last))
    def _():
        prepare(0)

    def forward_copy(tick, c):
        return pltpu.make_async_remote_copy(
            src_ref=forward_out.at[tick, c],
            dst_ref=forward_in.at[tick, c],
            send_sem=forward_send.at[tick, c],
            recv_sem=forward_recv.at[tick, c],
            device_id={"section": section + 1},
        )

    def backward_copy(tick, c):
        return pltpu.make_async_remote_copy(
            src_ref=backward_out.at[tick, c],
            dst_ref=backward_in.at[tick, c],
            send_sem=backward_send.at[tick, c],
            recv_sem=backward_recv.at[tick, c],
            device_id={"section": section - 1},
        )

    def forward(tick):
        product = jnp.zeros((FOLD * ROWS, FOLD * RANK), jnp.float32)
        total = jnp.zeros((ROWS, 128), jnp.float32)
        arrives = jnp.logical_and(tick > 0, jnp.logical_not(is_first))
        for c in range(CHUNKS):

            @pl.when(arrives)
            def _(c=c):
                forward_copy(tick, c).wait_recv()
                base = fold_rows(stored, slots[tick], c)
                bound = spread(bounds(exps_in[tick - 1]), c)
                step = clip_to(forward_in[tick, c].astype(jnp.float32) - base, bound)
                x_now[c] = (base + step.astype(jnp.bfloat16).astype(jnp.float32)).astype(jnp.bfloat16)

            @pl.when(jnp.logical_not(arrives))
            def _(c=c):
                x_now[c] = fold_rows(stored, slots[tick], c).astype(jnp.bfloat16)

            x = x_now[c]
            product = product + dot(x, weights[0, c], NT)
            total = total + squares(x.astype(jnp.float32))
        inverse, before, gate = row_stats(product, total)
        hidden = scatter_groups(before * gate)

        @pl.when(is_last)
        def _():
            keep_stats(inverse, before, gate)
            back_now[...] = x_now[...]

        @pl.when(tick == 0)
        def _():
            for offset in range(1, PARTS):
                weight_arrival(1, offset).wait_recv()

        for c in range(CHUNKS):
            output = x_now[c].astype(jnp.float32) + dot(hidden, weights[1, c], NN)

            @pl.when(jnp.logical_and(tick < ticks - 1, jnp.logical_not(is_last)))
            def _(c=c, output=output):
                forward_out[tick + 1, c] = output.astype(jnp.bfloat16)
                forward_copy(tick + 1, c).start()

            @pl.when(is_last)
            def _(c=c, output=output):
                distance = output - fold_rows(stored, slots[tick], c)
                backward_in[tick, c] = distance.astype(jnp.bfloat16)

            @pl.when(tick == ticks - 1)
            def _(c=c, output=output):
                @pl.when(is_last)
                def _():
                    copy_in[c] = fold_rows(stored, slots[tick], c).astype(jnp.bfloat16)

                distance = output - copy_in[c].astype(jnp.float32)
                delta = clip_to(distance, spread(bounds(delta_exp[tick]), c)).astype(jnp.bfloat16)
                for q in range(FOLD):
                    lanes = pl.ds(q * CHUNKS * LANES + c * LANES, LANES)
                    delta_out[:, lanes] = delta[q * ROWS : (q + 1) * ROWS]

    def share_copy(tick, offset):
        return pltpu.make_async_remote_copy(
            src_ref=shares_out.at[tick, peer(offset)],
            dst_ref=shares_in.at[tick, me],
            send_sem=share_send.at[tick],
            recv_sem=share_recv.at[tick],
            device_id={"dp": peer(offset)},
        )

    def all_shares(tick):
        return pltpu.make_async_remote_copy(
            src_ref=shares_out.at[tick, pl.ds(0, PARTS - 1)],
            dst_ref=shares_in.at[tick, pl.ds(0, PARTS - 1)],
            send_sem=share_send.at[tick],
            recv_sem=share_recv.at[tick],
            device_id={"dp": peer(1)},
        )

    def backward(tick):
        product = jnp.zeros((FOLD * ROWS, FOLD * RANK), jnp.float32)
        arrives = jnp.logical_and(tick > 0, jnp.logical_not(is_last))
        for c in range(CHUNKS):

            @pl.when(arrives)
            def _(c=c):
                backward_copy(tick, c).wait_recv()

            product = product + dot(backward_in[tick, c], weights[1, c], NT)
        inverse = stats[0]
        slope = gather_groups(product) * stats[2] * inverse
        pull = lane_total(slope * stats[1]) * (0.5 / features) * inverse
        pull = jnp.concatenate([jnp.concatenate([pull] * (LANES // 128), axis=1)] * FOLD, axis=0)
        spread_slope = scatter_groups(slope * SCALE)

        @pl.when(jnp.logical_and(tick < ticks - 1, jnp.logical_not(is_first)))
        def _():
            for c in range(CHUNKS):
                through = dot(spread_slope, weights[0, c], NN)
                result = backward_in[tick, c].astype(jnp.float32) + through - back_now[c].astype(jnp.float32) * pull
                bound = spread(bounds(grad_exp[tick]), c)
                backward_out[tick + 1, c] = clip_to(result, bound).astype(jnp.bfloat16)
                backward_copy(tick + 1, c).start()

        low = low_half()
        zero = jnp.zeros((ROWS, 128), jnp.float32)
        tail = jnp.concatenate([jnp.where(low, slope, zero), jnp.where(low, zero, stats[3])], axis=0).astype(jnp.bfloat16)
        for c in range(CHUNKS):
            back = back_now[c].astype(jnp.float32)
            cotangent = backward_in[tick, c].astype(jnp.float32)
            for q in range(FOLD):
                rows = slice(q * ROWS, (q + 1) * ROWS)
                pair = jnp.concatenate([back[rows], cotangent[rows]], axis=0)
                shares_out[tick, q * CHUNKS + c, :, 0:LANES] = pair.astype(jnp.bfloat16)
                shares_out[tick, q * CHUNKS + c, :, LANES : LANES + 128] = tail
        for offset in range(1, PARTS):
            share_copy(tick, offset).start()
        shares_in[tick, me] = shares_out[tick, me]

    def add_shares(tick):
        all_shares(tick).wait_recv()
        both = shares_in[tick].reshape(PARTS * 2 * ROWS, LANES + 128)
        totals[...] += dot(both[:, LANES:], both[:, :LANES], TN)

    def one_tick(tick, carry):
        forward(tick)
        backward(tick)

        @pl.when(jnp.logical_and(tick < ticks - 1, jnp.logical_not(is_last)))
        def _():
            prepare(tick + 1)

        @pl.when(tick == 0)
        def _():
            @pl.when(jnp.logical_not(is_first))
            def _():
                exps_copy.wait_recv()

            @pl.when(jnp.logical_not(is_last))
            def _():
                copy_copy.wait_recv()

        @pl.when(tick >= 2)
        def _():
            add_shares(tick - 2)

        return carry

    lax.fori_loop(0, ticks, one_tick, 0)
    add_shares(ticks - 2)
    add_shares(ticks - 1)

    factor = 1.0 / (ticks * ROWS)
    down_out[...] = (totals[0:RANK] * (own_gain * factor)).astype(jnp.bfloat16)
    up_out[...] = (totals[RANK : 2 * RANK] * factor).astype(jnp.bfloat16)

    for which in range(2):
        for offset in range(1, PARTS):
            weight_copy(which, offset).wait_send()

    @pl.when(jnp.logical_not(is_last))
    def _():
        exps_copy.wait_send()

        def drain(tick, carry):
            for c in range(CHUNKS):
                forward_copy(tick, c).wait_send()
            return carry

        lax.fori_loop(1, ticks, drain, 0)

    @pl.when(jnp.logical_not(is_first))
    def _():
        copy_copy.wait_send()

        def drain(tick, carry):
            for c in range(CHUNKS):
                backward_copy(tick, c).wait_send()
            return carry

        lax.fori_loop(1, ticks, drain, 0)

    def drain_shares(tick, carry):
        all_shares(tick).wait_send()
        return carry

    lax.fori_loop(0, ticks, drain_shares, 0)


def per_device(stored_inputs, slot_ids, incoming, delta_exp, grad_exp, norm_gain, down_weight, up_weight):
    stored = stored_inputs[0, 0]
    ticks = delta_exp.shape[2]
    sections = lax.axis_size("section")
    slot_count, rows, features = stored.shape
    message = (CHUNKS, FOLD * ROWS, LANES)
    bf16, f32 = jnp.bfloat16, jnp.float32
    vmem = pl.BlockSpec(memory_space=pltpu.VMEM)
    down_grad, up_grad, delta = pl.pallas_call(
        functools.partial(kernel, ticks, sections),
        out_shape=(
            jax.ShapeDtypeStruct((RANK, LANES), bf16),
            jax.ShapeDtypeStruct((RANK, LANES), bf16),
            jax.ShapeDtypeStruct((rows, features), bf16),
        ),
        in_specs=[pl.BlockSpec(memory_space=pltpu.SMEM), pl.BlockSpec(memory_space=pl.ANY)] + [vmem] * 6,
        out_specs=(vmem, vmem, vmem),
        scratch_shapes=[
            pltpu.VMEM((slot_count, rows, features), bf16),
            pltpu.VMEM((2, CHUNKS, FOLD * RANK, LANES), bf16),
            pltpu.VMEM((ticks,) + message, bf16),
            pltpu.VMEM((ticks,) + message, bf16),
            pltpu.VMEM((ticks,) + message, bf16),
            pltpu.VMEM((ticks,) + message, bf16),
            pltpu.VMEM((ticks, PARTS, 2 * ROWS, LANES + 128), bf16),
            pltpu.VMEM((ticks, PARTS, 2 * ROWS, LANES + 128), bf16),
            pltpu.VMEM(delta_exp.shape[2:], jnp.int32),
            pltpu.VMEM(message, bf16),
            pltpu.VMEM(message, bf16),
            pltpu.VMEM(message, bf16),
            pltpu.VMEM(message, bf16),
            pltpu.VMEM((4, ROWS, 128), f32),
            pltpu.VMEM((2 * RANK, LANES), f32),
            pltpu.SemaphoreType.DMA,
            pltpu.SemaphoreType.DMA((2, PARTS)),
            pltpu.SemaphoreType.DMA((2, PARTS)),
            pltpu.SemaphoreType.DMA((ticks, CHUNKS)),
            pltpu.SemaphoreType.DMA((ticks, CHUNKS)),
            pltpu.SemaphoreType.DMA((ticks, CHUNKS)),
            pltpu.SemaphoreType.DMA((ticks, CHUNKS)),
            pltpu.SemaphoreType.DMA((ticks,)),
            pltpu.SemaphoreType.DMA((ticks,)),
            pltpu.SemaphoreType.DMA((2,)),
            pltpu.SemaphoreType.DMA((2,)),
        ],
        compiler_params=pltpu.CompilerParams(
            collective_id=0, has_side_effects=True, vmem_limit_bytes=52 * 1024 * 1024
        ),
        name="relay",
    )(
        slot_ids[0, 0],
        stored,
        incoming[0, 0],
        delta_exp[0, 0],
        grad_exp[0, 0],
        norm_gain,
        down_weight[0].T,
        up_weight[0],
    )
    return down_grad.T[None], up_grad[None], delta[None, None]


def solution(mesh):
    return jax.shard_map(
        per_device,
        mesh=mesh,
        in_specs=(
            P("section", "dp", None, None, None),
            P("section", "dp", None),
            P("section", "dp", None, None),
            P("section", "dp", None, None, None),
            P("section", "dp", None, None, None),
            P("section", None),
            P("section", "dp", None),
            P("section", None, "dp"),
        ),
        out_specs=(
            P("section", "dp", None),
            P("section", None, "dp"),
            P("section", "dp", None, None),
        ),
        check_vma=False,
    )
```

```python
import functools

import jax
import jax.numpy as jnp
from jax import lax
from jax.experimental import pallas as pl
from jax.experimental.pallas import tpu as pltpu
from jax.sharding import PartitionSpec as P

EPSILON = 1e-05
PARTS = 16
CHIPS = 8
FOLD = 4
CHUNKS = 4
LANES = 512
ROWS = 8
RANK = 64
SCALE = 1024.0
NT = (((1,), (1,)), ((), ()))
TN = (((0,), (0,)), ((), ()))
NN = (((1,), (0,)), ((), ()))


def dot(a, b, dims):
    return lax.dot_general(a, b, dims, preferred_element_type=jnp.float32)


def bounds(exponent):
    return jnp.where(
        exponent == -7,
        127.0 * 2.0**-7,
        jnp.where(exponent == -6, 127.0 * 2.0**-6, jnp.where(exponent == -5, 127.0 * 2.0**-5, 127.0 * 2.0**-4)),
    ).astype(jnp.float32)


def spread(table, c):
    per = LANES // 128
    groups = []
    for q in range(FOLD):
        first = q * CHUNKS * per + c * per
        groups.append(
            jnp.concatenate(
                [jnp.broadcast_to(table[:, b : b + 1], (ROWS, 128)) for b in range(first, first + per)], axis=1
            )
        )
    return jnp.concatenate(groups, axis=0)


def clip_to(values, bound):
    return jnp.minimum(jnp.maximum(values, -bound), bound)


def fold_rows(ref, index, c):
    width = CHUNKS * LANES
    parts = []
    for q in range(FOLD):
        lanes = pl.ds(q * width + c * LANES, LANES)
        part = ref[:, lanes] if index is None else ref[index, :, lanes]
        parts.append(part.astype(jnp.float32))
    return jnp.concatenate(parts, axis=0)


def low_half():
    return lax.broadcasted_iota(jnp.int32, (ROWS, 128), 1) < RANK


def gather_groups(product):
    low = low_half()
    first = jnp.where(low, product[0:8, 0:128], product[8:16, 0:128])
    second = jnp.where(low, product[16:24, 128:256], product[24:32, 128:256])
    half = first + second
    return half + pltpu.roll(half, RANK, 1)


def scatter_groups(values):
    low = low_half()
    zero = jnp.zeros_like(values)
    left = jnp.where(low, values, zero)
    right = jnp.where(low, zero, values)
    first = jnp.concatenate([left, right, zero, zero], axis=0)
    second = jnp.concatenate([zero, zero, left, right], axis=0)
    return jnp.concatenate([first, second], axis=1).astype(jnp.bfloat16)


def lane_total(values):
    return jnp.broadcast_to(jnp.sum(values, axis=1, keepdims=True), (ROWS, 128))


def squares(x):
    total = jnp.zeros((ROWS, 128), jnp.float32)
    for q in range(FOLD):
        for i in range(LANES // 128):
            piece = x[q * ROWS : (q + 1) * ROWS, i * 128 : (i + 1) * 128]
            total = total + piece * piece
    return total


def kernel(
    ticks,
    sections,
    slots_hbm,
    stored_hbm,
    incoming_hbm,
    delta_exp_hbm,
    grad_exp_hbm,
    gain_hbm,
    down_hbm,
    up_hbm,
    down_out,
    up_out,
    delta_out,
    slots,
    stored,
    incoming,
    delta_exp,
    grad_exp,
    gain,
    down,
    up,
    weights,
    turned,
    forward_in,
    forward_out,
    backward_in,
    backward_out,
    shares_out,
    shares_in,
    exps_in,
    copy_out,
    copy_in,
    back_rows,
    back_squares,
    back_products,
    stats,
    forward_bound,
    backward_bound,
    totals,
    operand_sem,
    weight_send,
    weight_recv,
    forward_send,
    forward_recv,
    backward_send,
    backward_recv,
    share_send,
    share_recv,
    side_send,
    side_recv,
):
    section = lax.axis_index("section")
    me = lax.axis_index("dp")
    is_first = section == 0
    is_last = section == sections - 1
    not_first = section > 0
    not_last = section < sections - 1
    features = gain.shape[1]

    pairs = (
        (down_hbm, down),
        (up_hbm, up),
        (gain_hbm, gain),
        (delta_exp_hbm, delta_exp),
        (slots_hbm, slots),
        (stored_hbm, stored),
        (grad_exp_hbm, grad_exp),
        (incoming_hbm, incoming),
    )
    loads = [pltpu.make_async_copy(source, target, operand_sem.at[i]) for i, (source, target) in enumerate(pairs)]
    for load in loads:
        load.start()

    barrier = pltpu.get_barrier_semaphore()

    def peer(offset):
        return lax.rem(me + offset, PARTS)

    for offset in range(1, PARTS):
        pl.semaphore_signal(barrier, inc=1, device_id={"dp": peer(offset)})

    @pl.when(not_first)
    def _():
        pl.semaphore_signal(barrier, inc=1, device_id={"section": section - 1})

    @pl.when(not_last)
    def _():
        pl.semaphore_signal(barrier, inc=1, device_id={"section": section + 1})

    core = lax.rem(me, 2)
    chip = me // 2
    mate = me + 1 - 2 * core

    def block(which, owner):
        rows = pl.ds(pl.multiple_of((owner // CHUNKS) * RANK, RANK), RANK)
        return weights.at[which, lax.rem(owner, CHUNKS), rows, :]

    own_lanes = pl.ds(pl.multiple_of(me * LANES, LANES), LANES)
    for i in range(4):
        loads[i].wait()
    own_gain = gain[:, own_lanes]
    block(0, me)[...] = (down[...].astype(jnp.float32) * (own_gain * (1.0 / SCALE))).astype(jnp.bfloat16)
    block(1, me)[...] = up[...]

    ends = jnp.where(is_first, 1, 0) + jnp.where(is_last, 1, 0)
    pl.semaphore_wait(barrier, PARTS + 1 - ends)

    def block_copy(which, owner, send, to):
        return pltpu.make_async_remote_copy(
            src_ref=block(which, owner),
            dst_ref=block(which, owner),
            send_sem=weight_send.at[which, send],
            recv_sem=weight_recv.at[which, owner],
            device_id={"dp": to},
        )

    def chip_copy(which, offset):
        return block_copy(which, me, offset, lax.rem(chip + offset, CHIPS) * 2 + core)

    def mate_copy(which, offset):
        return block_copy(which, lax.rem(chip + CHIPS - offset, CHIPS) * 2 + core, CHIPS + offset, mate)

    def from_mate(which, offset):
        return block_copy(which, lax.rem(chip + CHIPS - offset, CHIPS) * 2 + 1 - core, CHIPS + offset, mate)

    for which in range(2):
        mate_copy(which, 0).start()
        for offset in range(1, CHIPS):
            chip_copy(which, offset).start()

    exps_copy = pltpu.make_async_remote_copy(
        src_ref=delta_exp,
        dst_ref=exps_in,
        send_sem=side_send.at[0],
        recv_sem=side_recv.at[0],
        device_id={"section": section + 1},
    )
    copy_copy = pltpu.make_async_remote_copy(
        src_ref=copy_out,
        dst_ref=copy_in,
        send_sem=side_send.at[1],
        recv_sem=side_recv.at[1],
        device_id={"section": section - 1},
    )

    @pl.when(not_last)
    def _():
        exps_copy.start()

    for load in loads[4:]:
        load.wait()

    @pl.when(not_first)
    def _():
        for c in range(CHUNKS):
            copy_out[c] = fold_rows(stored, slots[ticks], c).astype(jnp.bfloat16)
        copy_copy.start()

    @pl.when(is_last)
    def _():
        for c in range(CHUNKS):
            copy_in[c] = fold_rows(stored, slots[ticks - 1], c).astype(jnp.bfloat16)

    @pl.when(is_first)
    def _():
        exps_in[...] = delta_exp[...]

        def clear(tick, carry):
            forward_in[tick] = jnp.zeros(forward_in.shape[1:], jnp.bfloat16)
            return carry

        lax.fori_loop(0, ticks, clear, 0)

    totals[...] = jnp.zeros_like(totals)
    for c in range(CHUNKS):
        backward_in[0, c] = fold_rows(incoming, None, c).astype(jnp.bfloat16)

    def take_rows(tick, carry):
        slot = slots[jnp.where(tick == ticks, 0, ticks + 1 + tick)]
        total = jnp.zeros((ROWS, 128), jnp.float32)
        for c in range(CHUNKS):
            rows = fold_rows(stored, slot, c)
            back_rows[tick, c] = rows.astype(jnp.bfloat16)
            total = total + squares(rows)
        back_squares[tick] = total
        return carry

    lax.fori_loop(0, ticks + 1, take_rows, 0)

    def spread_back(tick, carry):
        table = bounds(grad_exp[tick])
        for c in range(CHUNKS):
            backward_bound[tick, c] = spread(table, c)
        return carry

    lax.fori_loop(0, ticks - 1, spread_back, 0)

    for offset in range(1, CHIPS):
        mate_copy(0, offset).wait_recv()
        mate_copy(0, offset).start()

    @pl.when(not_first)
    def _():
        exps_copy.wait_recv()

    own_table = bounds(delta_exp[ticks - 1])
    for c in range(CHUNKS):
        forward_bound[0, c] = spread(own_table, c)

    def spread_forward(tick, carry):
        table = bounds(exps_in[tick - 1]) * jnp.where(is_first, 0.0, 1.0)
        for c in range(CHUNKS):
            forward_bound[tick, c] = spread(table, c)
        return carry

    lax.fori_loop(1, ticks, spread_forward, 0)

    for offset in range(CHIPS):
        from_mate(0, offset).wait_recv()

    back_products[...] = jnp.zeros_like(back_products)

    def multiply(c, carry):
        rows = back_rows[:, c].reshape((ticks + 1) * FOLD * ROWS, LANES)
        back_products[...] += dot(rows, weights[0, c], NT)
        return carry

    lax.fori_loop(0, CHUNKS, multiply, 0)

    for offset in range(1, CHIPS):
        mate_copy(1, offset).wait_recv()
        mate_copy(1, offset).start()

    def row_stats(product, total):
        inverse = lax.rsqrt(lane_total(total) * (1.0 / features) + EPSILON)
        before = gather_groups(product) * (inverse * SCALE)
        gate = 1.0 / (1.0 + jnp.exp(-before))
        return inverse, before, gate

    def keep_stats(tick, inverse, before, gate):
        stats[tick, 0] = inverse
        stats[tick, 1] = before
        stats[tick, 2] = gate * (1.0 + before * (1.0 - gate))
        stats[tick, 3] = before * gate

    def back_stats(tick):
        first = tick * FOLD * ROWS
        if not isinstance(tick, int):
            first = pl.multiple_of(first, FOLD * ROWS)
        keep_stats(tick, *row_stats(back_products[pl.ds(first, FOLD * ROWS)], back_squares[tick]))

    back_stats(ticks)

    def four_stats(group, carry):
        for i in range(4):
            back_stats(group * 4 + i)
        return carry

    lax.fori_loop(0, ticks // 4, four_stats, 0)

    for offset in range(CHIPS):
        from_mate(1, offset).wait_recv()

    def forward_copy(tick, c):
        return pltpu.make_async_remote_copy(
            src_ref=forward_out.at[tick, c],
            dst_ref=forward_in.at[tick, c],
            send_sem=forward_send.at[tick, c],
            recv_sem=forward_recv.at[tick, c],
            device_id={"section": section + 1},
        )

    def backward_copy(tick, c):
        return pltpu.make_async_remote_copy(
            src_ref=backward_out.at[tick, c],
            dst_ref=backward_in.at[tick, c],
            send_sem=backward_send.at[tick, c],
            recv_sem=backward_recv.at[tick, c],
            device_id={"section": section - 1},
        )

    def forward(tick, begin, final):
        if begin:
            hidden = stats[ticks, 3]
        else:
            product = jnp.zeros((FOLD * ROWS, FOLD * RANK), jnp.float32)
            total = jnp.zeros((ROWS, 128), jnp.float32)
            for c in range(CHUNKS):

                @pl.when(not_first)
                def _(c=c):
                    forward_copy(tick, c).wait_recv()

                base = fold_rows(stored, slots[tick], c)
                step = clip_to(forward_in[tick, c].astype(jnp.float32) - base, forward_bound[tick, c])
                x = (base + step.astype(jnp.bfloat16).astype(jnp.float32)).astype(jnp.bfloat16)
                back_rows[ticks, c] = x
                product = product + dot(x, turned[0, c], NN)
                total = total + squares(x.astype(jnp.float32))
            inverse, before, gate = row_stats(product, total)
            keep_stats(ticks, inverse, before, gate)
            hidden = before * gate
        hidden = scatter_groups(hidden)
        for c in range(CHUNKS):
            output = back_rows[ticks, c].astype(jnp.float32) + dot(hidden, weights[1, c], NN)
            if final:
                delta = clip_to(output - copy_in[c].astype(jnp.float32), forward_bound[0, c]).astype(jnp.bfloat16)
                for q in range(FOLD):
                    lanes = pl.ds(q * CHUNKS * LANES + c * LANES, LANES)
                    delta_out[:, lanes] = delta[q * ROWS : (q + 1) * ROWS]
            else:
                forward_out[tick + 1, c] = output.astype(jnp.bfloat16)

                @pl.when(not_last)
                def _(c=c):
                    forward_copy(tick + 1, c).start()

        @pl.when(is_last)
        def _():
            for c in range(CHUNKS):
                output = back_rows[ticks, c].astype(jnp.float32) + dot(hidden, weights[1, c], NN)
                distance = output - fold_rows(stored, slots[tick], c)
                backward_in[ticks, c] = distance.astype(jnp.bfloat16)

    def share_copy(pair, offset):
        return pltpu.make_async_remote_copy(
            src_ref=shares_out.at[pair, peer(offset)],
            dst_ref=shares_in.at[pair, me],
            send_sem=share_send.at[pair],
            recv_sem=share_recv.at[pair],
            device_id={"dp": peer(offset)},
        )

    def all_shares(pair):
        return pltpu.make_async_remote_copy(
            src_ref=shares_out.at[pair, pl.ds(0, PARTS - 1)],
            dst_ref=shares_in.at[pair, pl.ds(0, PARTS - 1)],
            send_sem=share_send.at[pair],
            recv_sem=share_recv.at[pair],
            device_id={"dp": peer(1)},
        )

    def backward(tick, begin, final, pair, half):
        here = jnp.where(is_last, ticks, tick)
        product = jnp.zeros((FOLD * ROWS, FOLD * RANK), jnp.float32)
        for c in range(CHUNKS):
            if not begin:

                @pl.when(not_last)
                def _(c=c):
                    backward_copy(tick, c).wait_recv()

            cotangent = backward_in[here, c]
            if begin:
                product = product + dot(cotangent, weights[1, c], NT)
            else:
                product = product + dot(cotangent, turned[1, c], NN)
        inverse = stats[here, 0]
        slope = gather_groups(product) * stats[here, 2] * inverse
        if not final:
            pull = lane_total(slope * stats[here, 1]) * (0.5 / features) * inverse
            pull = jnp.concatenate([jnp.concatenate([pull] * (LANES // 128), axis=1)] * FOLD, axis=0)
            spread_slope = scatter_groups(slope * SCALE)
            for c in range(CHUNKS):
                through = dot(spread_slope, weights[0, c], NN)
                result = backward_in[here, c].astype(jnp.float32) + through
                result = result - back_rows[here, c].astype(jnp.float32) * pull
                backward_out[tick + 1, c] = clip_to(result, backward_bound[tick, c]).astype(jnp.bfloat16)

                @pl.when(not_first)
                def _(c=c):
                    backward_copy(tick + 1, c).start()

        low = low_half()
        zero = jnp.zeros((ROWS, 128), jnp.float32)
        tail = jnp.concatenate([jnp.where(low, slope, zero), jnp.where(low, zero, stats[here, 3])], axis=0)
        tail = tail.astype(jnp.bfloat16)
        for c in range(CHUNKS):
            back = back_rows[here, c].astype(jnp.float32)
            cotangent = backward_in[here, c].astype(jnp.float32)
            for q in range(FOLD):
                rows = slice(q * ROWS, (q + 1) * ROWS)
                both = jnp.concatenate([back[rows], cotangent[rows]], axis=0)
                shares_out[pair, q * CHUNKS + c, half, :, 0:LANES] = both.astype(jnp.bfloat16)
                shares_out[pair, q * CHUNKS + c, half, :, LANES : LANES + 128] = tail

    def send_shares(pair):
        for offset in range(1, PARTS):
            share_copy(pair, offset).start()
        shares_in[pair, me] = shares_out[pair, me]

    def add_shares(pair):
        all_shares(pair).wait_recv()
        both = shares_in[pair].reshape(PARTS * 4 * ROWS, LANES + 128)
        totals[...] += dot(both[:, LANES:], both[:, :LANES], TN)

    forward(0, True, False)
    backward(0, True, False, 0, 0)
    for which in range(2):
        for c in range(CHUNKS):
            turned[which, c] = weights[which, c].T

    def two_ticks(pair, carry):
        tick = 2 * pair + 1
        forward(tick, False, False)
        backward(tick, False, False, pair, 1)
        send_shares(pair)
        forward(tick + 1, False, False)
        backward(tick + 1, False, False, pair + 1, 0)

        @pl.when(pair >= 1)
        def _():
            add_shares(pair - 1)

        return carry

    lax.fori_loop(0, ticks // 2 - 1, two_ticks, 0)

    @pl.when(not_last)
    def _():
        copy_copy.wait_recv()

    forward(ticks - 1, False, True)
    backward(ticks - 1, False, True, ticks // 2 - 1, 1)
    send_shares(ticks // 2 - 1)
    add_shares(ticks // 2 - 2)

    for which in range(2):
        mate_copy(which, 0).wait_send()
        for offset in range(1, CHIPS):
            chip_copy(which, offset).wait_send()
            mate_copy(which, offset).wait_send()

    @pl.when(not_last)
    def _():
        exps_copy.wait_send()

        def drain(tick, carry):
            for c in range(CHUNKS):
                forward_copy(tick, c).wait_send()
            return carry

        lax.fori_loop(1, ticks, drain, 0)

    @pl.when(not_first)
    def _():
        copy_copy.wait_send()

        def drain(tick, carry):
            for c in range(CHUNKS):
                backward_copy(tick, c).wait_send()
            return carry

        lax.fori_loop(1, ticks, drain, 0)

    add_shares(ticks // 2 - 1)
    factor = 1.0 / (ticks * ROWS)
    down_out[...] = (totals[0:RANK] * (own_gain * factor)).astype(jnp.bfloat16)
    up_out[...] = (totals[RANK : 2 * RANK] * factor).astype(jnp.bfloat16)

    def drain_shares(pair, carry):
        all_shares(pair).wait_send()
        return carry

    lax.fori_loop(0, ticks // 2, drain_shares, 0)


def per_device(stored_inputs, slot_ids, incoming, delta_exp, grad_exp, norm_gain, down_weight, up_weight):
    stored = stored_inputs[0, 0]
    ticks = delta_exp.shape[2]
    sections = lax.axis_size("section")
    message = (CHUNKS, FOLD * ROWS, LANES)
    bf16, f32 = jnp.bfloat16, jnp.float32
    vmem = pl.BlockSpec(memory_space=pltpu.VMEM)
    operands = (
        slot_ids[0, 0],
        stored,
        incoming[0, 0],
        delta_exp[0, 0],
        grad_exp[0, 0],
        norm_gain,
        down_weight[0].T,
        up_weight[0],
    )
    shares = (ticks // 2, PARTS, 2, 2 * ROWS, LANES + 128)
    down_grad, up_grad, delta = pl.pallas_call(
        functools.partial(kernel, ticks, sections),
        out_shape=(
            jax.ShapeDtypeStruct((RANK, LANES), bf16),
            jax.ShapeDtypeStruct((RANK, LANES), bf16),
            jax.ShapeDtypeStruct(stored.shape[1:], bf16),
        ),
        in_specs=[pl.BlockSpec(memory_space=pl.ANY)] * len(operands),
        out_specs=(vmem, vmem, vmem),
        scratch_shapes=[pltpu.SMEM(operands[0].shape, jnp.int32)]
        + [pltpu.VMEM(operand.shape, operand.dtype) for operand in operands[1:]]
        + [
            pltpu.VMEM((2, CHUNKS, FOLD * RANK, LANES), bf16),
            pltpu.VMEM((2, CHUNKS, LANES, FOLD * RANK), bf16),
            pltpu.VMEM((ticks,) + message, bf16),
            pltpu.VMEM((ticks,) + message, bf16),
            pltpu.VMEM((ticks + 1,) + message, bf16),
            pltpu.VMEM((ticks,) + message, bf16),
            pltpu.VMEM(shares, bf16),
            pltpu.VMEM(shares, bf16),
            pltpu.VMEM(delta_exp.shape[2:], jnp.int32),
            pltpu.VMEM(message, bf16),
            pltpu.VMEM(message, bf16),
            pltpu.VMEM((ticks + 1,) + message, bf16),
            pltpu.VMEM((ticks + 1, ROWS, 128), f32),
            pltpu.VMEM(((ticks + 1) * FOLD * ROWS, FOLD * RANK), f32),
            pltpu.VMEM((ticks + 1, 4, ROWS, 128), f32),
            pltpu.VMEM((ticks,) + message, f32),
            pltpu.VMEM((ticks - 1,) + message, f32),
            pltpu.VMEM((2 * RANK, LANES), f32),
            pltpu.SemaphoreType.DMA((len(operands),)),
            pltpu.SemaphoreType.DMA((2, 2 * CHIPS)),
            pltpu.SemaphoreType.DMA((2, PARTS)),
            pltpu.SemaphoreType.DMA((ticks, CHUNKS)),
            pltpu.SemaphoreType.DMA((ticks, CHUNKS)),
            pltpu.SemaphoreType.DMA((ticks, CHUNKS)),
            pltpu.SemaphoreType.DMA((ticks, CHUNKS)),
            pltpu.SemaphoreType.DMA((ticks // 2,)),
            pltpu.SemaphoreType.DMA((ticks // 2,)),
            pltpu.SemaphoreType.DMA((2,)),
            pltpu.SemaphoreType.DMA((2,)),
        ],
        compiler_params=pltpu.CompilerParams(
            collective_id=0, has_side_effects=True, vmem_limit_bytes=56 * 1024 * 1024
        ),
        name="relay",
    )(*operands)
    return down_grad.T[None], up_grad[None], delta[None, None]


def solution(mesh):
    return jax.shard_map(
        per_device,
        mesh=mesh,
        in_specs=(
            P("section", "dp", None, None, None),
            P("section", "dp", None),
            P("section", "dp", None, None),
            P("section", "dp", None, None, None),
            P("section", "dp", None, None, None),
            P("section", None),
            P("section", "dp", None),
            P("section", None, "dp"),
        ),
        out_specs=(
            P("section", "dp", None),
            P("section", None, "dp"),
            P("section", "dp", None, None),
        ),
        check_vma=False,
    )
```

```python
import functools

import jax
import jax.numpy as jnp
from jax import lax
from jax.experimental import pallas as pl
from jax.experimental.pallas import tpu as pltpu
from jax.sharding import PartitionSpec as P

EPSILON = 1e-05
PARTS = 16
CHIPS = 8
FOLD = 4
CHUNKS = 4
LANES = 512
ROWS = 8
RANK = 64
SCALE = 1024.0
NT = (((1,), (1,)), ((), ()))
TN = (((0,), (0,)), ((), ()))
NN = (((1,), (0,)), ((), ()))


def dot(a, b, dims):
    return lax.dot_general(a, b, dims, preferred_element_type=jnp.float32)


def dot_in(a, b):
    half = a.shape[1] // 2
    return dot(a[:, :half], b[:half], NN), dot(a[:, half:], b[half:], NN)


def dot_out(a, b):
    half = b.shape[1] // 2
    return jnp.concatenate([dot(a, b[:, :half], NN), dot(a, b[:, half:], NN)], axis=1)


def bounds(exponent):
    return jnp.where(
        exponent == -7,
        127.0 * 2.0**-7,
        jnp.where(exponent == -6, 127.0 * 2.0**-6, jnp.where(exponent == -5, 127.0 * 2.0**-5, 127.0 * 2.0**-4)),
    ).astype(jnp.float32)


def spread(table, c):
    per = LANES // 128
    groups = []
    for q in range(FOLD):
        first = q * CHUNKS * per + c * per
        groups.append(
            jnp.concatenate(
                [jnp.broadcast_to(table[:, b : b + 1], (ROWS, 128)) for b in range(first, first + per)], axis=1
            )
        )
    return jnp.concatenate(groups, axis=0)


def clip_to(values, bound):
    return jnp.minimum(jnp.maximum(values, -bound), bound)


def fold_rows(ref, index, c):
    width = CHUNKS * LANES
    parts = []
    for q in range(FOLD):
        lanes = pl.ds(q * width + c * LANES, LANES)
        part = ref[:, lanes] if index is None else ref[index, :, lanes]
        parts.append(part.astype(jnp.float32))
    return jnp.concatenate(parts, axis=0)


def low_half():
    return lax.broadcasted_iota(jnp.int32, (ROWS, 128), 1) < RANK


def gather_groups(product):
    low = low_half()
    first = jnp.where(low, product[0:8, 0:128], product[8:16, 0:128])
    second = jnp.where(low, product[16:24, 128:256], product[24:32, 128:256])
    half = first + second
    return half + pltpu.roll(half, RANK, 1)


def scatter_groups(values):
    low = low_half()
    zero = jnp.zeros_like(values)
    left = jnp.where(low, values, zero)
    right = jnp.where(low, zero, values)
    first = jnp.concatenate([left, right, zero, zero], axis=0)
    second = jnp.concatenate([zero, zero, left, right], axis=0)
    return jnp.concatenate([first, second], axis=1).astype(jnp.bfloat16)


def lane_total(values):
    return jnp.broadcast_to(jnp.sum(values, axis=1, keepdims=True), (ROWS, 128))


def squares(x):
    total = jnp.zeros((ROWS, 128), jnp.float32)
    for q in range(FOLD):
        for i in range(LANES // 128):
            piece = x[q * ROWS : (q + 1) * ROWS, i * 128 : (i + 1) * 128]
            total = total + piece * piece
    return total


def kernel(
    ticks,
    sections,
    slots_hbm,
    stored_hbm,
    incoming_hbm,
    delta_exp_hbm,
    grad_exp_hbm,
    gain_hbm,
    down_hbm,
    up_hbm,
    down_out,
    up_out,
    delta_out,
    slots,
    stored,
    incoming,
    delta_exp,
    grad_exp,
    gain,
    down,
    up,
    weights,
    turned,
    forward_in,
    forward_out,
    backward_in,
    backward_out,
    shares_out,
    shares_in,
    exps_in,
    copy_out,
    copy_in,
    back_rows,
    back_squares,
    back_products,
    stats,
    forward_bound,
    backward_bound,
    totals,
    operand_sem,
    weight_send,
    weight_recv,
    forward_send,
    forward_recv,
    backward_send,
    backward_recv,
    share_send,
    share_recv,
    side_send,
    side_recv,
):
    section = lax.axis_index("section")
    me = lax.axis_index("dp")
    is_first = section == 0
    is_last = section == sections - 1
    not_first = section > 0
    not_last = section < sections - 1
    features = gain.shape[1]
    is_lower = section < sections // 2
    is_upper = section >= sections // 2
    lag = jnp.where(is_lower, 1, 0)

    pairs = (
        (down_hbm, down),
        (up_hbm, up),
        (gain_hbm, gain),
        (delta_exp_hbm, delta_exp),
        (slots_hbm, slots),
        (stored_hbm, stored),
        (grad_exp_hbm, grad_exp),
        (incoming_hbm, incoming),
    )
    loads = [pltpu.make_async_copy(source, target, operand_sem.at[i]) for i, (source, target) in enumerate(pairs)]
    for load in loads:
        load.start()

    barrier = pltpu.get_barrier_semaphore()

    def peer(offset):
        return lax.rem(me + offset, PARTS)

    for offset in range(1, PARTS):
        pl.semaphore_signal(barrier, inc=1, device_id={"dp": peer(offset)})

    @pl.when(not_first)
    def _():
        pl.semaphore_signal(barrier, inc=1, device_id={"section": section - 1})

    @pl.when(not_last)
    def _():
        pl.semaphore_signal(barrier, inc=1, device_id={"section": section + 1})

    core = lax.rem(me, 2)
    chip = me // 2
    mate = me + 1 - 2 * core

    def block(which, owner):
        rows = pl.ds(pl.multiple_of((owner // CHUNKS) * RANK, RANK), RANK)
        return weights.at[which, lax.rem(owner, CHUNKS), rows, :]

    own_lanes = pl.ds(pl.multiple_of(me * LANES, LANES), LANES)
    for i in range(4):
        loads[i].wait()
    own_gain = gain[:, own_lanes]
    block(0, me)[...] = (down[...].astype(jnp.float32) * (own_gain * (1.0 / SCALE))).astype(jnp.bfloat16)
    block(1, me)[...] = up[...]

    ends = jnp.where(is_first, 1, 0) + jnp.where(is_last, 1, 0)
    pl.semaphore_wait(barrier, PARTS + 1 - ends)

    def block_copy(which, owner, send, to):
        return pltpu.make_async_remote_copy(
            src_ref=block(which, owner),
            dst_ref=block(which, owner),
            send_sem=weight_send.at[which, send],
            recv_sem=weight_recv.at[which, owner],
            device_id={"dp": to},
        )

    def chip_copy(which, offset):
        return block_copy(which, me, offset, lax.rem(chip + offset, CHIPS) * 2 + core)

    def mate_copy(which, offset):
        return block_copy(which, lax.rem(chip + CHIPS - offset, CHIPS) * 2 + core, CHIPS + offset, mate)

    def from_mate(which, offset):
        return block_copy(which, lax.rem(chip + CHIPS - offset, CHIPS) * 2 + 1 - core, CHIPS + offset, mate)

    for which in range(2):
        mate_copy(which, 0).start()
        for offset in range(1, CHIPS):
            chip_copy(which, offset).start()

    exps_copy = pltpu.make_async_remote_copy(
        src_ref=delta_exp,
        dst_ref=exps_in,
        send_sem=side_send.at[0],
        recv_sem=side_recv.at[0],
        device_id={"section": section + 1},
    )
    copy_copy = pltpu.make_async_remote_copy(
        src_ref=copy_out,
        dst_ref=copy_in,
        send_sem=side_send.at[1],
        recv_sem=side_recv.at[1],
        device_id={"section": section - 1},
    )

    @pl.when(not_last)
    def _():
        exps_copy.start()

    for load in loads[4:]:
        load.wait()

    @pl.when(not_first)
    def _():
        for c in range(CHUNKS):
            copy_out[c] = fold_rows(stored, slots[ticks], c).astype(jnp.bfloat16)
        copy_copy.start()

    @pl.when(is_last)
    def _():
        for c in range(CHUNKS):
            copy_in[c] = fold_rows(stored, slots[ticks - 1], c).astype(jnp.bfloat16)

    @pl.when(is_first)
    def _():
        exps_in[...] = delta_exp[...]

        def clear(tick, carry):
            forward_in[tick] = jnp.zeros(forward_in.shape[1:], jnp.bfloat16)
            return carry

        lax.fori_loop(0, ticks, clear, 0)

    totals[...] = jnp.zeros_like(totals)
    for c in range(CHUNKS):
        backward_in[0, c] = fold_rows(incoming, None, c).astype(jnp.bfloat16)

    def take_rows(tick, carry):
        slot = slots[jnp.where(tick == ticks, 0, ticks + 1 + tick)]
        total = jnp.zeros((ROWS, 128), jnp.float32)
        for c in range(CHUNKS):
            rows = fold_rows(stored, slot, c)
            back_rows[tick, c] = rows.astype(jnp.bfloat16)
            total = total + squares(rows)
        back_squares[tick] = total
        return carry

    lax.fori_loop(0, ticks + 1, take_rows, 0)

    def spread_back(tick):
        table = bounds(grad_exp[tick])
        for c in range(CHUNKS):
            backward_bound[c] = spread(table, c)

    spread_back(0)

    for offset in range(1, CHIPS):
        mate_copy(0, offset).wait_recv()
        mate_copy(0, offset).start()

    @pl.when(not_first)
    def _():
        exps_copy.wait_recv()

    def spread_forward(tick, final):
        if final:
            table = bounds(delta_exp[tick])
        else:
            table = bounds(exps_in[tick]) * jnp.where(is_first, 0.0, 1.0)
        for c in range(CHUNKS):
            forward_bound[1 if final else 0, c] = spread(table, c)

    for offset in range(CHIPS):
        from_mate(0, offset).wait_recv()

    back_products[...] = jnp.zeros_like(back_products)

    def multiply(c, carry):
        rows = back_rows[:, c].reshape((ticks + 1) * FOLD * ROWS, LANES)
        back_products[...] += dot(rows, weights[0, c], NT)
        return carry

    lax.fori_loop(0, CHUNKS, multiply, 0)

    for offset in range(1, CHIPS):
        mate_copy(1, offset).wait_recv()
        mate_copy(1, offset).start()

    def row_stats(product, total):
        inverse = lax.rsqrt(lane_total(total) * (1.0 / features) + EPSILON)
        before = gather_groups(product) * (inverse * SCALE)
        gate = 1.0 / (1.0 + jnp.exp(-before))
        return inverse, before, gate

    def keep_stats(tick, inverse, before, gate):
        stats[tick, 0] = inverse
        stats[tick, 1] = before
        stats[tick, 2] = gate * (1.0 + before * (1.0 - gate))
        stats[tick, 3] = before * gate

    def back_stats(tick):
        first = tick * FOLD * ROWS
        if not isinstance(tick, int):
            first = pl.multiple_of(first, FOLD * ROWS)
        keep_stats(tick, *row_stats(back_products[pl.ds(first, FOLD * ROWS)], back_squares[tick]))

    back_stats(ticks)

    def four_stats(group, carry):
        for i in range(4):
            back_stats(group * 4 + i)
        return carry

    lax.fori_loop(0, ticks // 4, four_stats, 0)

    for offset in range(CHIPS):
        from_mate(1, offset).wait_recv()

    def forward_copy(tick, c):
        return pltpu.make_async_remote_copy(
            src_ref=forward_out.at[tick, c],
            dst_ref=forward_in.at[tick, c],
            send_sem=forward_send.at[tick, c],
            recv_sem=forward_recv.at[tick, c],
            device_id={"section": section + 1},
        )

    def backward_copy(tick, c):
        return pltpu.make_async_remote_copy(
            src_ref=backward_out.at[tick, c],
            dst_ref=backward_in.at[tick, c],
            send_sem=backward_send.at[tick, c],
            recv_sem=backward_recv.at[tick, c],
            device_id={"section": section - 1},
        )

    def forward(tick, begin, final):
        if begin:
            hidden = stats[ticks, 3]
        else:
            sums = [jnp.zeros((FOLD * ROWS, FOLD * RANK), jnp.float32)] * 2
            total = jnp.zeros((ROWS, 128), jnp.float32)
            for c in range(CHUNKS):

                @pl.when(not_first)
                def _(c=c):
                    forward_copy(tick, c).wait_recv()

                base = fold_rows(stored, slots[tick], c)
                step = clip_to(forward_in[tick, c].astype(jnp.float32) - base, forward_bound[0, c])
                x = (base + step.astype(jnp.bfloat16).astype(jnp.float32)).astype(jnp.bfloat16)
                back_rows[ticks, c] = x
                sums = [a + b for a, b in zip(sums, dot_in(x, turned[0, c]))]
                total = total + squares(x.astype(jnp.float32))
            inverse, before, gate = row_stats(sums[0] + sums[1], total)
            keep_stats(ticks, inverse, before, gate)
            hidden = before * gate
        hidden = scatter_groups(hidden)
        if not final:
            for c in range(CHUNKS):
                output = back_rows[ticks, c].astype(jnp.float32) + dot_out(hidden, weights[1, c])
                forward_out[tick + 1, c] = output.astype(jnp.bfloat16)

                @pl.when(not_last)
                def _(c=c):
                    forward_copy(tick + 1, c).start()

        @pl.when(is_last)
        def _():
            for c in range(CHUNKS):
                output = back_rows[ticks, c].astype(jnp.float32) + dot_out(hidden, weights[1, c])
                distance = output - fold_rows(stored, slots[tick], c)
                backward_in[ticks, c] = distance.astype(jnp.bfloat16)

        return hidden

    def give_delta(hidden):
        for c in range(CHUNKS):
            output = back_rows[ticks, c].astype(jnp.float32) + dot_out(hidden, weights[1, c])
            delta = clip_to(output - copy_in[c].astype(jnp.float32), forward_bound[1, c]).astype(jnp.bfloat16)
            for q in range(FOLD):
                lanes = pl.ds(q * CHUNKS * LANES + c * LANES, LANES)
                delta_out[:, lanes] = delta[q * ROWS : (q + 1) * ROWS]

    def share_copy(pair, offset):
        return pltpu.make_async_remote_copy(
            src_ref=shares_out.at[pair, peer(offset)],
            dst_ref=shares_in.at[pair, me],
            send_sem=share_send.at[pair],
            recv_sem=share_recv.at[pair],
            device_id={"dp": peer(offset)},
        )

    def all_shares(pair):
        return pltpu.make_async_remote_copy(
            src_ref=shares_out.at[pair, pl.ds(0, PARTS - 1)],
            dst_ref=shares_in.at[pair, pl.ds(0, PARTS - 1)],
            send_sem=share_send.at[pair],
            recv_sem=share_recv.at[pair],
            device_id={"dp": peer(1)},
        )

    def backward(tick, begin, final):
        pair, half = tick // 2, lax.rem(tick, 2)
        here = jnp.where(is_last, ticks, tick)
        sums = [jnp.zeros((FOLD * ROWS, FOLD * RANK), jnp.float32)] * 2
        for c in range(CHUNKS):
            if not begin:

                @pl.when(jnp.logical_and(not_last, tick > 0))
                def _(c=c):
                    backward_copy(tick, c).wait_recv()

            cotangent = backward_in[here, c]
            if begin:
                sums[0] = sums[0] + dot(cotangent, weights[1, c], NT)
            else:
                sums = [a + b for a, b in zip(sums, dot_in(cotangent, turned[1, c]))]
        inverse = stats[here, 0]
        slope = gather_groups(sums[0] + sums[1]) * stats[here, 2] * inverse
        if not final:
            pull = lane_total(slope * stats[here, 1]) * (0.5 / features) * inverse
            pull = jnp.concatenate([jnp.concatenate([pull] * (LANES // 128), axis=1)] * FOLD, axis=0)
            spread_slope = scatter_groups(slope * SCALE)
            for c in range(CHUNKS):
                through = dot_out(spread_slope, weights[0, c])
                result = backward_in[here, c].astype(jnp.float32) + through
                result = result - back_rows[here, c].astype(jnp.float32) * pull
                backward_out[tick + 1, c] = clip_to(result, backward_bound[c]).astype(jnp.bfloat16)

                @pl.when(not_first)
                def _(c=c):
                    backward_copy(tick + 1, c).start()

        low = low_half()
        zero = jnp.zeros((ROWS, 128), jnp.float32)
        tail = jnp.concatenate([jnp.where(low, slope, zero), jnp.where(low, zero, stats[here, 3])], axis=0)
        tail = tail.astype(jnp.bfloat16)
        for c in range(CHUNKS):
            back = back_rows[here, c].astype(jnp.float32)
            cotangent = backward_in[here, c].astype(jnp.float32)
            for q in range(FOLD):
                rows = slice(q * ROWS, (q + 1) * ROWS)
                both = jnp.concatenate([back[rows], cotangent[rows]], axis=0)
                shares_out[pair, q * CHUNKS + c, half, :, 0:LANES] = both.astype(jnp.bfloat16)
                shares_out[pair, q * CHUNKS + c, half, :, LANES : LANES + 128] = tail

    def send_shares(pair):
        for offset in range(1, PARTS):
            share_copy(pair, offset).start()
        shares_in[pair, me] = shares_out[pair, me]

    def add_shares(pair):
        all_shares(pair).wait_recv()
        both = shares_in[pair].reshape(PARTS * 4 * ROWS, LANES + 128)
        totals[...] += dot(both[:, LANES:], both[:, :LANES], TN)

    forward(0, True, False)

    @pl.when(is_upper)
    def _():
        backward(0, True, False)
        spread_back(1)

    spread_forward(0, False)
    for which in range(2):
        for c in range(CHUNKS):
            turned[which, c] = weights[which, c].T

    def two_ticks(pair, carry):
        tick = 2 * pair + 1
        forward(tick, False, False)
        backward(tick - lag, False, False)
        spread_forward(tick, False)
        spread_back(tick + 1 - lag)

        @pl.when(is_upper)
        def _():
            send_shares(pair)

        forward(tick + 1, False, False)
        backward(tick + 1 - lag, False, False)
        spread_forward(tick + 1, False)
        spread_back(jnp.minimum(tick + 2 - lag, ticks - 2))

        @pl.when(is_lower)
        def _():
            send_shares(pair)

        @pl.when(pair >= 1)
        def _():
            add_shares(pair - 1)

        return carry

    lax.fori_loop(0, ticks // 2 - 1, two_ticks, 0)

    @pl.when(not_last)
    def _():
        copy_copy.wait_recv()

    spread_forward(ticks - 1, True)
    last_hidden = forward(ticks - 1, False, True)

    @pl.when(is_lower)
    def _():
        backward(ticks - 2, False, False)

    backward(ticks - 1, False, True)
    send_shares(ticks // 2 - 1)
    give_delta(last_hidden)
    add_shares(ticks // 2 - 2)

    for which in range(2):
        mate_copy(which, 0).wait_send()
        for offset in range(1, CHIPS):
            chip_copy(which, offset).wait_send()
            mate_copy(which, offset).wait_send()

    @pl.when(not_last)
    def _():
        exps_copy.wait_send()

        def drain(tick, carry):
            for c in range(CHUNKS):
                forward_copy(tick, c).wait_send()
            return carry

        lax.fori_loop(1, ticks, drain, 0)

    @pl.when(not_first)
    def _():
        copy_copy.wait_send()

        def drain(tick, carry):
            for c in range(CHUNKS):
                backward_copy(tick, c).wait_send()
            return carry

        lax.fori_loop(1, ticks, drain, 0)

    add_shares(ticks // 2 - 1)
    factor = 1.0 / (ticks * ROWS)
    down_out[...] = (totals[0:RANK] * (own_gain * factor)).astype(jnp.bfloat16)
    up_out[...] = (totals[RANK : 2 * RANK] * factor).astype(jnp.bfloat16)

    def drain_shares(pair, carry):
        all_shares(pair).wait_send()
        return carry

    lax.fori_loop(0, ticks // 2, drain_shares, 0)


def per_device(stored_inputs, slot_ids, incoming, delta_exp, grad_exp, norm_gain, down_weight, up_weight):
    stored = stored_inputs[0, 0]
    ticks = delta_exp.shape[2]
    sections = lax.axis_size("section")
    message = (CHUNKS, FOLD * ROWS, LANES)
    bf16, f32 = jnp.bfloat16, jnp.float32
    vmem = pl.BlockSpec(memory_space=pltpu.VMEM)
    operands = (
        slot_ids[0, 0],
        stored,
        incoming[0, 0],
        delta_exp[0, 0],
        grad_exp[0, 0],
        norm_gain,
        down_weight[0].T,
        up_weight[0],
    )
    shares = (ticks // 2, PARTS, 2, 2 * ROWS, LANES + 128)
    down_grad, up_grad, delta = pl.pallas_call(
        functools.partial(kernel, ticks, sections),
        out_shape=(
            jax.ShapeDtypeStruct((RANK, LANES), bf16),
            jax.ShapeDtypeStruct((RANK, LANES), bf16),
            jax.ShapeDtypeStruct(stored.shape[1:], bf16),
        ),
        in_specs=[pl.BlockSpec(memory_space=pl.ANY)] * len(operands),
        out_specs=(vmem, vmem, vmem),
        scratch_shapes=[pltpu.SMEM(operands[0].shape, jnp.int32)]
        + [pltpu.VMEM(operand.shape, operand.dtype) for operand in operands[1:]]
        + [
            pltpu.VMEM((2, CHUNKS, FOLD * RANK, LANES), bf16),
            pltpu.VMEM((2, CHUNKS, LANES, FOLD * RANK), bf16),
            pltpu.VMEM((ticks,) + message, bf16),
            pltpu.VMEM((ticks,) + message, bf16),
            pltpu.VMEM((ticks + 1,) + message, bf16),
            pltpu.VMEM((ticks,) + message, bf16),
            pltpu.VMEM(shares, bf16),
            pltpu.VMEM(shares, bf16),
            pltpu.VMEM(delta_exp.shape[2:], jnp.int32),
            pltpu.VMEM(message, bf16),
            pltpu.VMEM(message, bf16),
            pltpu.VMEM((ticks + 1,) + message, bf16),
            pltpu.VMEM((ticks + 1, ROWS, 128), f32),
            pltpu.VMEM(((ticks + 1) * FOLD * ROWS, FOLD * RANK), f32),
            pltpu.VMEM((ticks + 1, 4, ROWS, 128), f32),
            pltpu.VMEM((2,) + message, f32),
            pltpu.VMEM(message, f32),
            pltpu.VMEM((2 * RANK, LANES), f32),
            pltpu.SemaphoreType.DMA((len(operands),)),
            pltpu.SemaphoreType.DMA((2, 2 * CHIPS)),
            pltpu.SemaphoreType.DMA((2, PARTS)),
            pltpu.SemaphoreType.DMA((ticks, CHUNKS)),
            pltpu.SemaphoreType.DMA((ticks, CHUNKS)),
            pltpu.SemaphoreType.DMA((ticks, CHUNKS)),
            pltpu.SemaphoreType.DMA((ticks, CHUNKS)),
            pltpu.SemaphoreType.DMA((ticks // 2,)),
            pltpu.SemaphoreType.DMA((ticks // 2,)),
            pltpu.SemaphoreType.DMA((2,)),
            pltpu.SemaphoreType.DMA((2,)),
        ],
        compiler_params=pltpu.CompilerParams(
            collective_id=0, has_side_effects=True, vmem_limit_bytes=56 * 1024 * 1024
        ),
        name="relay",
    )(*operands)
    return down_grad.T[None], up_grad[None], delta[None, None]


def solution(mesh):
    return jax.shard_map(
        per_device,
        mesh=mesh,
        in_specs=(
            P("section", "dp", None, None, None),
            P("section", "dp", None),
            P("section", "dp", None, None),
            P("section", "dp", None, None, None),
            P("section", "dp", None, None, None),
            P("section", None),
            P("section", "dp", None),
            P("section", None, "dp"),
        ),
        out_specs=(
            P("section", "dp", None),
            P("section", None, "dp"),
            P("section", "dp", None, None),
        ),
        check_vma=False,
    )
```

```python
import functools

import jax
import jax.numpy as jnp
from jax import lax
from jax.experimental import pallas as pl
from jax.experimental.pallas import tpu as pltpu
from jax.sharding import PartitionSpec as P

EPSILON = 1e-05
PARTS = 16
CHIPS = 8
FOLD = 4
CHUNKS = 4
LANES = 512
ROWS = 8
RANK = 64
SCALE = 1024.0
NT = (((1,), (1,)), ((), ()))
TN = (((0,), (0,)), ((), ()))
NN = (((1,), (0,)), ((), ()))


def dot(a, b, dims):
    return lax.dot_general(a, b, dims, preferred_element_type=jnp.float32)


def dot_in(a, b):
    half = a.shape[1] // 2
    return dot(a[:, :half], b[:half], NN), dot(a[:, half:], b[half:], NN)


def dot_out(a, b):
    half = b.shape[1] // 2
    return jnp.concatenate([dot(a, b[:, :half], NN), dot(a, b[:, half:], NN)], axis=1)


def bounds(exponent):
    return jnp.where(
        exponent == -7,
        127.0 * 2.0**-7,
        jnp.where(exponent == -6, 127.0 * 2.0**-6, jnp.where(exponent == -5, 127.0 * 2.0**-5, 127.0 * 2.0**-4)),
    ).astype(jnp.float32)


def spread(table, c):
    per = LANES // 128
    groups = []
    for q in range(FOLD):
        first = q * CHUNKS * per + c * per
        groups.append(
            jnp.concatenate(
                [jnp.broadcast_to(table[:, b : b + 1], (ROWS, 128)) for b in range(first, first + per)], axis=1
            )
        )
    return jnp.concatenate(groups, axis=0)


def clip_to(values, bound):
    return jnp.minimum(jnp.maximum(values, -bound), bound)


def fold_rows(ref, index, c):
    width = CHUNKS * LANES
    parts = []
    for q in range(FOLD):
        lanes = pl.ds(q * width + c * LANES, LANES)
        part = ref[:, lanes] if index is None else ref[index, :, lanes]
        parts.append(part.astype(jnp.float32))
    return jnp.concatenate(parts, axis=0)


def low_half():
    return lax.broadcasted_iota(jnp.int32, (ROWS, 128), 1) < RANK


def gather_groups(product):
    low = low_half()
    first = jnp.where(low, product[0:8, 0:128], product[8:16, 0:128])
    second = jnp.where(low, product[16:24, 128:256], product[24:32, 128:256])
    half = first + second
    return half + pltpu.roll(half, RANK, 1)


def scatter_groups(values):
    low = low_half()
    zero = jnp.zeros_like(values)
    left = jnp.where(low, values, zero)
    right = jnp.where(low, zero, values)
    first = jnp.concatenate([left, right, zero, zero], axis=0)
    second = jnp.concatenate([zero, zero, left, right], axis=0)
    return jnp.concatenate([first, second], axis=1).astype(jnp.bfloat16)


def lane_total(values):
    return jnp.broadcast_to(jnp.sum(values, axis=1, keepdims=True), (ROWS, 128))


def squares(x):
    total = jnp.zeros((ROWS, 128), jnp.float32)
    for q in range(FOLD):
        for i in range(LANES // 128):
            piece = x[q * ROWS : (q + 1) * ROWS, i * 128 : (i + 1) * 128]
            total = total + piece * piece
    return total


def kernel(
    ticks,
    sections,
    slots_hbm,
    stored_hbm,
    incoming_hbm,
    delta_exp_hbm,
    grad_exp_hbm,
    gain_hbm,
    down_hbm,
    up_hbm,
    down_out,
    up_out,
    delta_out,
    slots,
    stored,
    incoming,
    delta_exp,
    grad_exp,
    gain,
    down,
    up,
    weights,
    turned,
    forward_in,
    forward_out,
    backward_in,
    backward_out,
    shares_out,
    shares_in,
    exps_in,
    copy_out,
    copy_in,
    back_rows,
    back_squares,
    back_products,
    stats,
    forward_bound,
    backward_bound,
    totals,
    sums_out,
    sums_in,
    operand_sem,
    weight_send,
    weight_recv,
    forward_send,
    forward_recv,
    backward_send,
    backward_recv,
    share_send,
    share_recv,
    side_send,
    side_recv,
):
    section = lax.axis_index("section")
    me = lax.axis_index("dp")
    is_first = section == 0
    is_last = section == sections - 1
    not_first = section > 0
    not_last = section < sections - 1
    features = gain.shape[1]
    is_lower = section < sections // 2
    is_upper = section >= sections // 2
    lag = jnp.where(is_lower, 1, 0)

    pairs = (
        (down_hbm, down),
        (up_hbm, up),
        (gain_hbm, gain),
        (delta_exp_hbm, delta_exp),
        (slots_hbm, slots),
        (stored_hbm, stored),
        (grad_exp_hbm, grad_exp),
        (incoming_hbm, incoming),
    )
    loads = [pltpu.make_async_copy(source, target, operand_sem.at[i]) for i, (source, target) in enumerate(pairs)]
    for load in loads:
        load.start()

    barrier = pltpu.get_barrier_semaphore()

    for offset in range(1, PARTS):
        pl.semaphore_signal(barrier, inc=1, device_id={"dp": lax.rem(me + offset, PARTS)})

    @pl.when(not_first)
    def _():
        pl.semaphore_signal(barrier, inc=1, device_id={"section": section - 1})

    @pl.when(not_last)
    def _():
        pl.semaphore_signal(barrier, inc=1, device_id={"section": section + 1})

    core = lax.rem(me, 2)
    chip = me // 2
    mate = me + 1 - 2 * core

    def block(which, owner):
        rows = pl.ds(pl.multiple_of((owner // CHUNKS) * RANK, RANK), RANK)
        return weights.at[which, lax.rem(owner, CHUNKS), rows, :]

    own_lanes = pl.ds(pl.multiple_of(me * LANES, LANES), LANES)
    for i in range(4):
        loads[i].wait()
    own_gain = gain[:, own_lanes]
    block(0, me)[...] = (down[...].astype(jnp.float32) * (own_gain * (1.0 / SCALE))).astype(jnp.bfloat16)
    block(1, me)[...] = up[...]

    ends = jnp.where(is_first, 1, 0) + jnp.where(is_last, 1, 0)
    pl.semaphore_wait(barrier, PARTS + 1 - ends)

    def block_copy(which, owner, send, to):
        return pltpu.make_async_remote_copy(
            src_ref=block(which, owner),
            dst_ref=block(which, owner),
            send_sem=weight_send.at[which, send],
            recv_sem=weight_recv.at[which, owner],
            device_id={"dp": to},
        )

    def chip_copy(which, offset):
        return block_copy(which, me, offset, lax.rem(chip + offset, CHIPS) * 2 + core)

    def mate_copy(which, offset):
        return block_copy(which, lax.rem(chip + CHIPS - offset, CHIPS) * 2 + core, CHIPS + offset, mate)

    def from_mate(which, offset):
        return block_copy(which, lax.rem(chip + CHIPS - offset, CHIPS) * 2 + 1 - core, CHIPS + offset, mate)

    for which in range(2):
        mate_copy(which, 0).start()
        for offset in range(1, CHIPS):
            chip_copy(which, offset).start()

    exps_copy = pltpu.make_async_remote_copy(
        src_ref=delta_exp,
        dst_ref=exps_in,
        send_sem=side_send.at[0],
        recv_sem=side_recv.at[0],
        device_id={"section": section + 1},
    )
    copy_copy = pltpu.make_async_remote_copy(
        src_ref=copy_out,
        dst_ref=copy_in,
        send_sem=side_send.at[1],
        recv_sem=side_recv.at[1],
        device_id={"section": section - 1},
    )

    @pl.when(not_last)
    def _():
        exps_copy.start()

    for load in loads[4:]:
        load.wait()

    @pl.when(not_first)
    def _():
        for c in range(CHUNKS):
            copy_out[c] = fold_rows(stored, slots[ticks], c).astype(jnp.bfloat16)
        copy_copy.start()

    @pl.when(is_last)
    def _():
        for c in range(CHUNKS):
            copy_in[c] = fold_rows(stored, slots[ticks - 1], c).astype(jnp.bfloat16)

    @pl.when(is_first)
    def _():
        exps_in[...] = delta_exp[...]

        def clear(tick, carry):
            forward_in[tick] = jnp.zeros(forward_in.shape[1:], jnp.bfloat16)
            return carry

        lax.fori_loop(0, ticks, clear, 0)

    totals[...] = jnp.zeros_like(totals)
    for c in range(CHUNKS):
        backward_in[0, c] = fold_rows(incoming, None, c).astype(jnp.bfloat16)

    def take_rows(tick, carry):
        slot = slots[jnp.where(tick == ticks, 0, ticks + 1 + tick)]
        total = jnp.zeros((ROWS, 128), jnp.float32)
        for c in range(CHUNKS):
            rows = fold_rows(stored, slot, c)
            back_rows[tick, c] = rows.astype(jnp.bfloat16)
            total = total + squares(rows)
        back_squares[tick] = total
        return carry

    lax.fori_loop(0, ticks + 1, take_rows, 0)

    def spread_back(tick):
        table = bounds(grad_exp[tick])
        for c in range(CHUNKS):
            backward_bound[c] = spread(table, c)

    spread_back(0)

    for offset in range(1, CHIPS):
        mate_copy(0, offset).wait_recv()
        mate_copy(0, offset).start()

    @pl.when(not_first)
    def _():
        exps_copy.wait_recv()

    def spread_forward(tick, final):
        if final:
            table = bounds(delta_exp[tick])
        else:
            table = bounds(exps_in[tick]) * jnp.where(is_first, 0.0, 1.0)
        for c in range(CHUNKS):
            forward_bound[1 if final else 0, c] = spread(table, c)

    for offset in range(CHIPS):
        from_mate(0, offset).wait_recv()

    back_products[...] = jnp.zeros_like(back_products)

    def multiply(c, carry):
        rows = back_rows[:, c].reshape((ticks + 1) * FOLD * ROWS, LANES)
        back_products[...] += dot(rows, weights[0, c], NT)
        return carry

    lax.fori_loop(0, CHUNKS, multiply, 0)

    for offset in range(1, CHIPS):
        mate_copy(1, offset).wait_recv()
        mate_copy(1, offset).start()

    def row_stats(product, total):
        inverse = lax.rsqrt(lane_total(total) * (1.0 / features) + EPSILON)
        before = gather_groups(product) * (inverse * SCALE)
        gate = 1.0 / (1.0 + jnp.exp(-before))
        return inverse, before, gate

    def keep_stats(tick, inverse, before, gate):
        stats[tick, 0] = inverse
        stats[tick, 1] = before
        stats[tick, 2] = gate * (1.0 + before * (1.0 - gate))
        stats[tick, 3] = before * gate

    def back_stats(tick):
        first = tick * FOLD * ROWS
        if not isinstance(tick, int):
            first = pl.multiple_of(first, FOLD * ROWS)
        keep_stats(tick, *row_stats(back_products[pl.ds(first, FOLD * ROWS)], back_squares[tick]))

    back_stats(ticks)

    def four_stats(group, carry):
        for i in range(4):
            back_stats(group * 4 + i)
        return carry

    lax.fori_loop(0, ticks // 4, four_stats, 0)

    for offset in range(CHIPS):
        from_mate(1, offset).wait_recv()

    def forward_copy(tick, c):
        return pltpu.make_async_remote_copy(
            src_ref=forward_out.at[tick, c],
            dst_ref=forward_in.at[tick, c],
            send_sem=forward_send.at[tick, c],
            recv_sem=forward_recv.at[tick, c],
            device_id={"section": section + 1},
        )

    def backward_copy(tick, c):
        return pltpu.make_async_remote_copy(
            src_ref=backward_out.at[tick, c],
            dst_ref=backward_in.at[tick, c],
            send_sem=backward_send.at[tick, c],
            recv_sem=backward_recv.at[tick, c],
            device_id={"section": section - 1},
        )

    def forward(tick, begin, final):
        if begin:
            hidden = stats[ticks, 3]
        else:
            sums = [jnp.zeros((FOLD * ROWS, FOLD * RANK), jnp.float32)] * 2
            total = jnp.zeros((ROWS, 128), jnp.float32)
            for c in range(CHUNKS):

                @pl.when(not_first)
                def _(c=c):
                    forward_copy(tick, c).wait_recv()

                base = fold_rows(stored, slots[tick], c)
                step = clip_to(forward_in[tick, c].astype(jnp.float32) - base, forward_bound[0, c])
                x = (base + step.astype(jnp.bfloat16).astype(jnp.float32)).astype(jnp.bfloat16)
                back_rows[ticks, c] = x
                sums = [a + b for a, b in zip(sums, dot_in(x, turned[0, c]))]
                total = total + squares(x.astype(jnp.float32))
            inverse, before, gate = row_stats(sums[0] + sums[1], total)
            keep_stats(ticks, inverse, before, gate)
            hidden = before * gate
        hidden = scatter_groups(hidden)
        if not final:
            for c in range(CHUNKS):
                output = back_rows[ticks, c].astype(jnp.float32) + dot_out(hidden, weights[1, c])
                forward_out[tick + 1, c] = output.astype(jnp.bfloat16)

                @pl.when(not_last)
                def _(c=c):
                    forward_copy(tick + 1, c).start()

        @pl.when(is_last)
        def _():
            for c in range(CHUNKS):
                output = back_rows[ticks, c].astype(jnp.float32) + dot_out(hidden, weights[1, c])
                distance = output - fold_rows(stored, slots[tick], c)
                backward_in[ticks, c] = distance.astype(jnp.bfloat16)

        return hidden

    def give_delta(hidden):
        for c in range(CHUNKS):
            output = back_rows[ticks, c].astype(jnp.float32) + dot_out(hidden, weights[1, c])
            delta = clip_to(output - copy_in[c].astype(jnp.float32), forward_bound[1, c]).astype(jnp.bfloat16)
            for q in range(FOLD):
                lanes = pl.ds(q * CHUNKS * LANES + c * LANES, LANES)
                delta_out[:, lanes] = delta[q * ROWS : (q + 1) * ROWS]

    side = lax.rem(me // 2, 2)
    number = (me // 4) * 2 + core

    def member(index, on_side):
        return (index // 2) * 4 + on_side * 2 + lax.rem(index, 2)

    def share_copy(pair, offset, other):
        to = lax.rem(number + offset, CHIPS)
        return pltpu.make_async_remote_copy(
            src_ref=shares_out.at[pair, member(to, 1 - side if other else side)],
            dst_ref=shares_in.at[pair, other, number],
            send_sem=share_send.at[pair],
            recv_sem=share_recv.at[pair],
            device_id={"dp": member(to, side)},
        )

    def all_shares(pair):
        seven = shares_in.at[pair, :, pl.ds(0, CHIPS - 1)]
        return pltpu.make_async_remote_copy(
            src_ref=seven,
            dst_ref=seven,
            send_sem=share_send.at[pair],
            recv_sem=share_recv.at[pair],
            device_id={"dp": member(lax.rem(number + 1, CHIPS), side)},
        )

    sums_copy = pltpu.make_async_remote_copy(
        src_ref=sums_out,
        dst_ref=sums_in,
        send_sem=side_send.at[2],
        recv_sem=side_recv.at[2],
        device_id={"dp": member(number, 1 - side)},
    )

    def backward(tick, begin, final):
        pair, half = tick // 2, lax.rem(tick, 2)
        here = jnp.where(is_last, ticks, tick)
        sums = [jnp.zeros((FOLD * ROWS, FOLD * RANK), jnp.float32)] * 2
        for c in range(CHUNKS):
            if not begin:

                @pl.when(jnp.logical_and(not_last, tick > 0))
                def _(c=c):
                    backward_copy(tick, c).wait_recv()

            cotangent = backward_in[here, c]
            if begin:
                sums[0] = sums[0] + dot(cotangent, weights[1, c], NT)
            else:
                sums = [a + b for a, b in zip(sums, dot_in(cotangent, turned[1, c]))]
        inverse = stats[here, 0]
        slope = gather_groups(sums[0] + sums[1]) * stats[here, 2] * inverse
        if not final:
            pull = lane_total(slope * stats[here, 1]) * (0.5 / features) * inverse
            pull = jnp.concatenate([jnp.concatenate([pull] * (LANES // 128), axis=1)] * FOLD, axis=0)
            spread_slope = scatter_groups(slope * SCALE)
            for c in range(CHUNKS):
                through = dot_out(spread_slope, weights[0, c])
                result = backward_in[here, c].astype(jnp.float32) + through
                result = result - back_rows[here, c].astype(jnp.float32) * pull
                backward_out[tick + 1, c] = clip_to(result, backward_bound[c]).astype(jnp.bfloat16)

                @pl.when(not_first)
                def _(c=c):
                    backward_copy(tick + 1, c).start()

        low = low_half()
        zero = jnp.zeros((ROWS, 128), jnp.float32)
        tail = jnp.concatenate([jnp.where(low, slope, zero), jnp.where(low, zero, stats[here, 3])], axis=0)
        tail = tail.astype(jnp.bfloat16)
        for c in range(CHUNKS):
            back = back_rows[here, c].astype(jnp.float32)
            cotangent = backward_in[here, c].astype(jnp.float32)
            for q in range(FOLD):
                rows = slice(q * ROWS, (q + 1) * ROWS)
                both = jnp.concatenate([back[rows], cotangent[rows]], axis=0)
                shares_out[pair, q * CHUNKS + c, half, :, 0:LANES] = both.astype(jnp.bfloat16)
                shares_out[pair, q * CHUNKS + c, half, :, LANES : LANES + 128] = tail

    def send_shares(pair):
        for offset in range(1, CHIPS):
            for other in range(2):
                share_copy(pair, offset, other).start()
        for other in range(2):
            shares_in[pair, other, number] = shares_out[pair, member(number, 1 - side if other else side)]

    def add_shares(pair):
        all_shares(pair).wait_recv()
        for other in range(2):
            both = shares_in[pair, other].reshape(CHIPS * 4 * ROWS, LANES + 128)
            totals[other] += dot(both[:, LANES:], both[:, :LANES], TN)

    forward(0, True, False)

    @pl.when(is_upper)
    def _():
        backward(0, True, False)
        spread_back(1)

    spread_forward(0, False)
    for which in range(2):
        for c in range(CHUNKS):
            turned[which, c] = weights[which, c].T

    def two_ticks(pair, carry):
        tick = 2 * pair + 1
        forward(tick, False, False)
        backward(tick - lag, False, False)
        spread_forward(tick, False)
        spread_back(tick + 1 - lag)

        @pl.when(is_upper)
        def _():
            send_shares(pair)

        forward(tick + 1, False, False)
        backward(tick + 1 - lag, False, False)
        spread_forward(tick + 1, False)
        spread_back(jnp.minimum(tick + 2 - lag, ticks - 2))

        @pl.when(is_lower)
        def _():
            send_shares(pair)

        @pl.when(pair >= 2)
        def _():
            add_shares(pair - 2)

        return carry

    lax.fori_loop(0, ticks // 2 - 1, two_ticks, 0)

    @pl.when(not_last)
    def _():
        copy_copy.wait_recv()

    spread_forward(ticks - 1, True)
    last_hidden = forward(ticks - 1, False, True)

    @pl.when(is_lower)
    def _():
        backward(ticks - 2, False, False)

    backward(ticks - 1, False, True)
    send_shares(ticks // 2 - 1)
    give_delta(last_hidden)
    for pair in range(max(ticks // 2 - 3, 0), ticks // 2):
        add_shares(pair)
    sums_out[...] = totals[1].astype(jnp.bfloat16)
    sums_copy.start()

    for which in range(2):
        mate_copy(which, 0).wait_send()
        for offset in range(1, CHIPS):
            chip_copy(which, offset).wait_send()
            mate_copy(which, offset).wait_send()

    @pl.when(not_last)
    def _():
        exps_copy.wait_send()

        def drain(tick, carry):
            for c in range(CHUNKS):
                forward_copy(tick, c).wait_send()
            return carry

        lax.fori_loop(1, ticks, drain, 0)

    @pl.when(not_first)
    def _():
        copy_copy.wait_send()

        def drain(tick, carry):
            for c in range(CHUNKS):
                backward_copy(tick, c).wait_send()
            return carry

        lax.fori_loop(1, ticks, drain, 0)

    sums_copy.wait()
    summed = totals[0] + sums_in[...].astype(jnp.float32)
    factor = 1.0 / (ticks * ROWS)
    down_out[...] = (summed[0:RANK] * (own_gain * factor)).astype(jnp.bfloat16)
    up_out[...] = (summed[RANK : 2 * RANK] * factor).astype(jnp.bfloat16)

    def drain_shares(pair, carry):
        all_shares(pair).wait_send()
        return carry

    lax.fori_loop(0, ticks // 2, drain_shares, 0)


def per_device(stored_inputs, slot_ids, incoming, delta_exp, grad_exp, norm_gain, down_weight, up_weight):
    stored = stored_inputs[0, 0]
    ticks = delta_exp.shape[2]
    sections = lax.axis_size("section")
    message = (CHUNKS, FOLD * ROWS, LANES)
    bf16, f32 = jnp.bfloat16, jnp.float32
    vmem = pl.BlockSpec(memory_space=pltpu.VMEM)
    operands = (
        slot_ids[0, 0],
        stored,
        incoming[0, 0],
        delta_exp[0, 0],
        grad_exp[0, 0],
        norm_gain,
        down_weight[0].T,
        up_weight[0],
    )
    shares = (ticks // 2, PARTS, 2, 2 * ROWS, LANES + 128)
    down_grad, up_grad, delta = pl.pallas_call(
        functools.partial(kernel, ticks, sections),
        out_shape=(
            jax.ShapeDtypeStruct((RANK, LANES), bf16),
            jax.ShapeDtypeStruct((RANK, LANES), bf16),
            jax.ShapeDtypeStruct(stored.shape[1:], bf16),
        ),
        in_specs=[pl.BlockSpec(memory_space=pl.ANY)] * len(operands),
        out_specs=(vmem, vmem, vmem),
        scratch_shapes=[pltpu.SMEM(operands[0].shape, jnp.int32)]
        + [pltpu.VMEM(operand.shape, operand.dtype) for operand in operands[1:]]
        + [
            pltpu.VMEM((2, CHUNKS, FOLD * RANK, LANES), bf16),
            pltpu.VMEM((2, CHUNKS, LANES, FOLD * RANK), bf16),
            pltpu.VMEM((ticks,) + message, bf16),
            pltpu.VMEM((ticks,) + message, bf16),
            pltpu.VMEM((ticks + 1,) + message, bf16),
            pltpu.VMEM((ticks,) + message, bf16),
            pltpu.VMEM(shares, bf16),
            pltpu.VMEM((ticks // 2, 2, CHIPS, 2, 2 * ROWS, LANES + 128), bf16),
            pltpu.VMEM(delta_exp.shape[2:], jnp.int32),
            pltpu.VMEM(message, bf16),
            pltpu.VMEM(message, bf16),
            pltpu.VMEM((ticks + 1,) + message, bf16),
            pltpu.VMEM((ticks + 1, ROWS, 128), f32),
            pltpu.VMEM(((ticks + 1) * FOLD * ROWS, FOLD * RANK), f32),
            pltpu.VMEM((ticks + 1, 4, ROWS, 128), f32),
            pltpu.VMEM((2,) + message, f32),
            pltpu.VMEM(message, f32),
            pltpu.VMEM((2, 2 * RANK, LANES), f32),
            pltpu.VMEM((2 * RANK, LANES), bf16),
            pltpu.VMEM((2 * RANK, LANES), bf16),
            pltpu.SemaphoreType.DMA((len(operands),)),
            pltpu.SemaphoreType.DMA((2, 2 * CHIPS)),
            pltpu.SemaphoreType.DMA((2, PARTS)),
            pltpu.SemaphoreType.DMA((ticks, CHUNKS)),
            pltpu.SemaphoreType.DMA((ticks, CHUNKS)),
            pltpu.SemaphoreType.DMA((ticks, CHUNKS)),
            pltpu.SemaphoreType.DMA((ticks, CHUNKS)),
            pltpu.SemaphoreType.DMA((ticks // 2,)),
            pltpu.SemaphoreType.DMA((ticks // 2,)),
            pltpu.SemaphoreType.DMA((3,)),
            pltpu.SemaphoreType.DMA((3,)),
        ],
        compiler_params=pltpu.CompilerParams(
            collective_id=0, has_side_effects=True, vmem_limit_bytes=56 * 1024 * 1024
        ),
        name="relay",
    )(*operands)
    return down_grad.T[None], up_grad[None], delta[None, None]


def solution(mesh):
    return jax.shard_map(
        per_device,
        mesh=mesh,
        in_specs=(
            P("section", "dp", None, None, None),
            P("section", "dp", None),
            P("section", "dp", None, None),
            P("section", "dp", None, None, None),
            P("section", "dp", None, None, None),
            P("section", None),
            P("section", "dp", None),
            P("section", None, "dp"),
        ),
        out_specs=(
            P("section", "dp", None),
            P("section", None, "dp"),
            P("section", "dp", None, None),
        ),
        check_vma=False,
    )
```

```python
import functools

import jax
import jax.numpy as jnp
from jax import lax
from jax.experimental import pallas as pl
from jax.experimental.pallas import tpu as pltpu
from jax.sharding import PartitionSpec as P

EPSILON = 1e-05
PARTS = 16
CHIPS = 8
FOLD = 4
CHUNKS = 4
LANES = 512
ROWS = 8
RANK = 64
SCALE = 1024.0
NT = (((1,), (1,)), ((), ()))
TN = (((0,), (0,)), ((), ()))
NN = (((1,), (0,)), ((), ()))


def dot(a, b, dims):
    return lax.dot_general(a, b, dims, preferred_element_type=jnp.float32)


def dot_in(a, b):
    half = a.shape[1] // 2
    return dot(a[:, :half], b[:half], NN), dot(a[:, half:], b[half:], NN)


def dot_out(a, b):
    half = b.shape[1] // 2
    return jnp.concatenate([dot(a, b[:, :half], NN), dot(a, b[:, half:], NN)], axis=1)


def bounds(exponent):
    return jnp.where(
        exponent == -7,
        127.0 * 2.0**-7,
        jnp.where(exponent == -6, 127.0 * 2.0**-6, jnp.where(exponent == -5, 127.0 * 2.0**-5, 127.0 * 2.0**-4)),
    ).astype(jnp.float32)


def spread(table, c):
    per = LANES // 128
    groups = []
    for q in range(FOLD):
        first = q * CHUNKS * per + c * per
        groups.append(
            jnp.concatenate(
                [jnp.broadcast_to(table[:, b : b + 1], (ROWS, 128)) for b in range(first, first + per)], axis=1
            )
        )
    return jnp.concatenate(groups, axis=0)


def clip_to(values, bound):
    return jnp.minimum(jnp.maximum(values, -bound), bound)


def fold_rows(ref, index, c):
    width = CHUNKS * LANES
    parts = []
    for q in range(FOLD):
        lanes = pl.ds(q * width + c * LANES, LANES)
        part = ref[:, lanes] if index is None else ref[index, :, lanes]
        parts.append(part.astype(jnp.float32))
    return jnp.concatenate(parts, axis=0)


def low_half():
    return lax.broadcasted_iota(jnp.int32, (ROWS, 128), 1) < RANK


def gather_groups(product):
    low = low_half()
    first = jnp.where(low, product[0:8, 0:128], product[8:16, 0:128])
    second = jnp.where(low, product[16:24, 128:256], product[24:32, 128:256])
    half = first + second
    return half + pltpu.roll(half, RANK, 1)


def scatter_groups(values):
    low = low_half()
    zero = jnp.zeros_like(values)
    left = jnp.where(low, values, zero)
    right = jnp.where(low, zero, values)
    first = jnp.concatenate([left, right, zero, zero], axis=0)
    second = jnp.concatenate([zero, zero, left, right], axis=0)
    return jnp.concatenate([first, second], axis=1).astype(jnp.bfloat16)


def lane_total(values):
    return jnp.broadcast_to(jnp.sum(values, axis=1, keepdims=True), (ROWS, 128))


def squares(x):
    total = jnp.zeros((ROWS, 128), jnp.float32)
    for q in range(FOLD):
        for i in range(LANES // 128):
            piece = x[q * ROWS : (q + 1) * ROWS, i * 128 : (i + 1) * 128]
            total = total + piece * piece
    return total


def kernel(
    ticks,
    sections,
    slots_hbm,
    stored_hbm,
    incoming_hbm,
    delta_exp_hbm,
    grad_exp_hbm,
    gain_hbm,
    down_hbm,
    up_hbm,
    down_out,
    up_out,
    delta_out,
    slots,
    stored,
    incoming,
    delta_exp,
    grad_exp,
    gain,
    down,
    up,
    weights,
    turned,
    forward_in,
    forward_out,
    backward_in,
    backward_out,
    shares_out,
    shares_in,
    last_in,
    exps_in,
    copy_out,
    copy_in,
    back_rows,
    back_squares,
    back_products,
    stats,
    forward_bound,
    backward_bound,
    totals,
    sums_out,
    sums_in,
    operand_sem,
    weight_send,
    weight_recv,
    forward_send,
    forward_recv,
    backward_send,
    backward_recv,
    share_send,
    share_recv,
    side_send,
    side_recv,
):
    section = lax.axis_index("section")
    me = lax.axis_index("dp")
    is_first = section == 0
    is_last = section == sections - 1
    not_first = section > 0
    not_last = section < sections - 1
    features = gain.shape[1]
    is_lower = section < sections // 2
    is_upper = section >= sections // 2
    lag = jnp.where(is_lower, 1, 0)

    pairs = (
        (down_hbm, down),
        (up_hbm, up),
        (gain_hbm, gain),
        (delta_exp_hbm, delta_exp),
        (slots_hbm, slots),
        (stored_hbm, stored),
        (grad_exp_hbm, grad_exp),
        (incoming_hbm, incoming),
    )
    loads = [pltpu.make_async_copy(source, target, operand_sem.at[i]) for i, (source, target) in enumerate(pairs)]
    for load in loads:
        load.start()

    barrier = pltpu.get_barrier_semaphore()

    for offset in range(1, PARTS):
        pl.semaphore_signal(barrier, inc=1, device_id={"dp": lax.rem(me + offset, PARTS)})

    @pl.when(not_first)
    def _():
        pl.semaphore_signal(barrier, inc=1, device_id={"section": section - 1})

    @pl.when(not_last)
    def _():
        pl.semaphore_signal(barrier, inc=1, device_id={"section": section + 1})

    core = lax.rem(me, 2)
    chip = me // 2
    mate = me + 1 - 2 * core

    def block(which, owner):
        rows = pl.ds(pl.multiple_of((owner // CHUNKS) * RANK, RANK), RANK)
        return weights.at[which, lax.rem(owner, CHUNKS), rows, :]

    own_lanes = pl.ds(pl.multiple_of(me * LANES, LANES), LANES)
    for i in range(4):
        loads[i].wait()
    own_gain = gain[:, own_lanes]
    block(0, me)[...] = (down[...].astype(jnp.float32) * (own_gain * (1.0 / SCALE))).astype(jnp.bfloat16)
    block(1, me)[...] = up[...]

    ends = jnp.where(is_first, 1, 0) + jnp.where(is_last, 1, 0)
    pl.semaphore_wait(barrier, PARTS + 1 - ends)

    def block_copy(which, owner, send, to):
        return pltpu.make_async_remote_copy(
            src_ref=block(which, owner),
            dst_ref=block(which, owner),
            send_sem=weight_send.at[which, send],
            recv_sem=weight_recv.at[which, owner],
            device_id={"dp": to},
        )

    def chip_copy(which, offset):
        return block_copy(which, me, offset, lax.rem(chip + offset, CHIPS) * 2 + core)

    def mate_copy(which, offset):
        return block_copy(which, lax.rem(chip + CHIPS - offset, CHIPS) * 2 + core, CHIPS + offset, mate)

    def from_mate(which, offset):
        return block_copy(which, lax.rem(chip + CHIPS - offset, CHIPS) * 2 + 1 - core, CHIPS + offset, mate)

    for which in range(2):
        mate_copy(which, 0).start()
        for offset in range(1, CHIPS):
            chip_copy(which, offset).start()

    exps_copy = pltpu.make_async_remote_copy(
        src_ref=delta_exp,
        dst_ref=exps_in,
        send_sem=side_send.at[0],
        recv_sem=side_recv.at[0],
        device_id={"section": section + 1},
    )
    copy_copy = pltpu.make_async_remote_copy(
        src_ref=copy_out,
        dst_ref=copy_in,
        send_sem=side_send.at[1],
        recv_sem=side_recv.at[1],
        device_id={"section": section - 1},
    )

    @pl.when(not_last)
    def _():
        exps_copy.start()

    for load in loads[4:]:
        load.wait()

    @pl.when(not_first)
    def _():
        for c in range(CHUNKS):
            copy_out[c] = fold_rows(stored, slots[ticks], c).astype(jnp.bfloat16)
        copy_copy.start()

    @pl.when(is_last)
    def _():
        for c in range(CHUNKS):
            copy_in[c] = fold_rows(stored, slots[ticks - 1], c).astype(jnp.bfloat16)

    @pl.when(is_first)
    def _():
        exps_in[...] = delta_exp[...]

        def clear(tick, carry):
            forward_in[tick] = jnp.zeros(forward_in.shape[1:], jnp.bfloat16)
            return carry

        lax.fori_loop(0, ticks, clear, 0)

    totals[...] = jnp.zeros_like(totals)
    for c in range(CHUNKS):
        backward_in[0, c] = fold_rows(incoming, None, c).astype(jnp.bfloat16)

    def take_rows(tick, carry):
        slot = slots[jnp.where(tick == ticks, 0, ticks + 1 + tick)]
        total = jnp.zeros((ROWS, 128), jnp.float32)
        for c in range(CHUNKS):
            rows = fold_rows(stored, slot, c)
            back_rows[tick, c] = rows.astype(jnp.bfloat16)
            total = total + squares(rows)
        back_squares[tick] = total
        return carry

    lax.fori_loop(0, ticks + 1, take_rows, 0)

    def spread_back(tick):
        table = bounds(grad_exp[tick])
        for c in range(CHUNKS):
            backward_bound[c] = spread(table, c)

    spread_back(0)

    for offset in range(1, CHIPS):
        mate_copy(0, offset).wait_recv()
        mate_copy(0, offset).start()

    @pl.when(not_first)
    def _():
        exps_copy.wait_recv()

    def spread_forward(tick, final):
        if final:
            table = bounds(delta_exp[tick])
        else:
            table = bounds(exps_in[tick]) * jnp.where(is_first, 0.0, 1.0)
        for c in range(CHUNKS):
            forward_bound[1 if final else 0, c] = spread(table, c)

    for offset in range(CHIPS):
        from_mate(0, offset).wait_recv()

    back_products[...] = jnp.zeros_like(back_products)

    def multiply(c, carry):
        rows = back_rows[:, c].reshape((ticks + 1) * FOLD * ROWS, LANES)
        back_products[...] += dot(rows, weights[0, c], NT)
        return carry

    lax.fori_loop(0, CHUNKS, multiply, 0)

    for offset in range(1, CHIPS):
        mate_copy(1, offset).wait_recv()
        mate_copy(1, offset).start()

    def row_stats(product, total):
        inverse = lax.rsqrt(lane_total(total) * (1.0 / features) + EPSILON)
        before = gather_groups(product) * (inverse * SCALE)
        gate = 1.0 / (1.0 + jnp.exp(-before))
        return inverse, before, gate

    def keep_stats(tick, inverse, before, gate):
        stats[tick, 0] = inverse
        stats[tick, 1] = before
        stats[tick, 2] = gate * (1.0 + before * (1.0 - gate))
        stats[tick, 3] = before * gate

    def back_stats(tick):
        first = tick * FOLD * ROWS
        if not isinstance(tick, int):
            first = pl.multiple_of(first, FOLD * ROWS)
        keep_stats(tick, *row_stats(back_products[pl.ds(first, FOLD * ROWS)], back_squares[tick]))

    back_stats(ticks)

    def four_stats(group, carry):
        for i in range(4):
            back_stats(group * 4 + i)
        return carry

    lax.fori_loop(0, ticks // 4, four_stats, 0)

    for offset in range(CHIPS):
        from_mate(1, offset).wait_recv()

    def forward_copy(tick, c):
        return pltpu.make_async_remote_copy(
            src_ref=forward_out.at[tick, c],
            dst_ref=forward_in.at[tick, c],
            send_sem=forward_send.at[tick, c],
            recv_sem=forward_recv.at[tick, c],
            device_id={"section": section + 1},
        )

    def backward_copy(tick, c):
        return pltpu.make_async_remote_copy(
            src_ref=backward_out.at[tick, c],
            dst_ref=backward_in.at[tick, c],
            send_sem=backward_send.at[tick, c],
            recv_sem=backward_recv.at[tick, c],
            device_id={"section": section - 1},
        )

    def forward(tick, begin, final):
        if begin:
            hidden = stats[ticks, 3]
        else:
            sums = [jnp.zeros((FOLD * ROWS, FOLD * RANK), jnp.float32)] * 2
            total = jnp.zeros((ROWS, 128), jnp.float32)
            for c in range(CHUNKS):

                @pl.when(not_first)
                def _(c=c):
                    forward_copy(tick, c).wait_recv()

                base = fold_rows(stored, slots[tick], c)
                step = clip_to(forward_in[tick, c].astype(jnp.float32) - base, forward_bound[0, c])
                x = (base + step.astype(jnp.bfloat16).astype(jnp.float32)).astype(jnp.bfloat16)
                back_rows[ticks, c] = x
                sums = [a + b for a, b in zip(sums, dot_in(x, turned[0, c]))]
                total = total + squares(x.astype(jnp.float32))
            inverse, before, gate = row_stats(sums[0] + sums[1], total)
            keep_stats(ticks, inverse, before, gate)
            hidden = before * gate
        hidden = scatter_groups(hidden)
        if not final:
            for c in range(CHUNKS):
                output = back_rows[ticks, c].astype(jnp.float32) + dot_out(hidden, weights[1, c])
                forward_out[tick + 1, c] = output.astype(jnp.bfloat16)

                @pl.when(not_last)
                def _(c=c):
                    forward_copy(tick + 1, c).start()

        @pl.when(is_last)
        def _():
            for c in range(CHUNKS):
                output = back_rows[ticks, c].astype(jnp.float32) + dot_out(hidden, weights[1, c])
                distance = output - fold_rows(stored, slots[tick], c)
                backward_in[ticks, c] = distance.astype(jnp.bfloat16)

        return hidden

    def give_delta(hidden):
        for c in range(CHUNKS):
            output = back_rows[ticks, c].astype(jnp.float32) + dot_out(hidden, weights[1, c])
            delta = clip_to(output - copy_in[c].astype(jnp.float32), forward_bound[1, c]).astype(jnp.bfloat16)
            for q in range(FOLD):
                lanes = pl.ds(q * CHUNKS * LANES + c * LANES, LANES)
                delta_out[:, lanes] = delta[q * ROWS : (q + 1) * ROWS]

    side = lax.rem(me // 2, 2)
    number = (me // 4) * 2 + core

    def member(index, on_side):
        return (index // 2) * 4 + on_side * 2 + lax.rem(index, 2)

    def share_copy(pair, offset, other):
        to = lax.rem(number + offset, CHIPS)
        return pltpu.make_async_remote_copy(
            src_ref=shares_out.at[pair, member(to, 1 - side if other else side)],
            dst_ref=shares_in.at[pair, other, number],
            send_sem=share_send.at[pair],
            recv_sem=share_recv.at[pair],
            device_id={"dp": member(to, side)},
        )

    def all_shares(pair):
        seven = shares_in.at[pair, :, pl.ds(0, CHIPS - 1)]
        return pltpu.make_async_remote_copy(
            src_ref=seven,
            dst_ref=seven,
            send_sem=share_send.at[pair],
            recv_sem=share_recv.at[pair],
            device_id={"dp": member(lax.rem(number + 1, CHIPS), side)},
        )

    last_pair = ticks // 2 - 1

    def first_copy(offset, other):
        to = lax.rem(number + offset, CHIPS)
        return pltpu.make_async_remote_copy(
            src_ref=shares_out.at[last_pair, member(to, 1 - side if other else side), 0],
            dst_ref=shares_in.at[last_pair, other, number, 0],
            send_sem=share_send.at[last_pair],
            recv_sem=share_recv.at[last_pair],
            device_id={"dp": member(to, side)},
        )

    def all_first():
        seven = shares_in.at[last_pair, :, pl.ds(0, CHIPS - 1), 0]
        return pltpu.make_async_remote_copy(
            src_ref=seven,
            dst_ref=seven,
            send_sem=share_send.at[last_pair],
            recv_sem=share_recv.at[last_pair],
            device_id={"dp": member(lax.rem(number + 1, CHIPS), side)},
        )

    def second_copy(offset):
        to = lax.rem(me + offset, PARTS)
        return pltpu.make_async_remote_copy(
            src_ref=shares_out.at[last_pair, to, 1],
            dst_ref=last_in.at[me],
            send_sem=share_send.at[last_pair + 1],
            recv_sem=share_recv.at[last_pair + 1],
            device_id={"dp": to},
        )

    def all_second():
        others = last_in.at[pl.ds(0, PARTS - 1)]
        return pltpu.make_async_remote_copy(
            src_ref=others,
            dst_ref=others,
            send_sem=share_send.at[last_pair + 1],
            recv_sem=share_recv.at[last_pair + 1],
            device_id={"dp": lax.rem(me + 1, PARTS)},
        )

    sums_copy = pltpu.make_async_remote_copy(
        src_ref=sums_out,
        dst_ref=sums_in,
        send_sem=side_send.at[2],
        recv_sem=side_recv.at[2],
        device_id={"dp": member(number, 1 - side)},
    )

    def backward(tick, begin, final):
        pair, half = tick // 2, lax.rem(tick, 2)
        here = jnp.where(is_last, ticks, tick)
        sums = [jnp.zeros((FOLD * ROWS, FOLD * RANK), jnp.float32)] * 2
        for c in range(CHUNKS):
            if not begin:

                @pl.when(jnp.logical_and(not_last, tick > 0))
                def _(c=c):
                    backward_copy(tick, c).wait_recv()

            cotangent = backward_in[here, c]
            if begin:
                sums[0] = sums[0] + dot(cotangent, weights[1, c], NT)
            else:
                sums = [a + b for a, b in zip(sums, dot_in(cotangent, turned[1, c]))]
        inverse = stats[here, 0]
        slope = gather_groups(sums[0] + sums[1]) * stats[here, 2] * inverse
        if not final:
            pull = lane_total(slope * stats[here, 1]) * (0.5 / features) * inverse
            pull = jnp.concatenate([jnp.concatenate([pull] * (LANES // 128), axis=1)] * FOLD, axis=0)
            spread_slope = scatter_groups(slope * SCALE)
            for c in range(CHUNKS):
                through = dot_out(spread_slope, weights[0, c])
                result = backward_in[here, c].astype(jnp.float32) + through
                result = result - back_rows[here, c].astype(jnp.float32) * pull
                backward_out[tick + 1, c] = clip_to(result, backward_bound[c]).astype(jnp.bfloat16)

                @pl.when(not_first)
                def _(c=c):
                    backward_copy(tick + 1, c).start()

        low = low_half()
        zero = jnp.zeros((ROWS, 128), jnp.float32)
        tail = jnp.concatenate([jnp.where(low, slope, zero), jnp.where(low, zero, stats[here, 3])], axis=0)
        tail = tail.astype(jnp.bfloat16)
        for c in range(CHUNKS):
            back = back_rows[here, c].astype(jnp.float32)
            cotangent = backward_in[here, c].astype(jnp.float32)
            for q in range(FOLD):
                rows = slice(q * ROWS, (q + 1) * ROWS)
                both = jnp.concatenate([back[rows], cotangent[rows]], axis=0)
                shares_out[pair, q * CHUNKS + c, half, :, 0:LANES] = both.astype(jnp.bfloat16)
                shares_out[pair, q * CHUNKS + c, half, :, LANES : LANES + 128] = tail

    def send_shares(pair):
        for offset in range(1, CHIPS):
            for other in range(2):
                share_copy(pair, offset, other).start()
        for other in range(2):
            shares_in[pair, other, number] = shares_out[pair, member(number, 1 - side if other else side)]

    def add_shares(pair):
        all_shares(pair).wait_recv()
        for other in range(2):
            both = shares_in[pair, other].reshape(CHIPS * 4 * ROWS, LANES + 128)
            totals[other] += dot(both[:, LANES:], both[:, :LANES], TN)

    def send_first():
        for offset in range(1, CHIPS):
            for other in range(2):
                first_copy(offset, other).start()
        for other in range(2):
            own = shares_out[last_pair, member(number, 1 - side if other else side), 0]
            shares_in[last_pair, other, number, 0] = own

    def add_first():
        all_first().wait_recv()
        for other in range(2):
            both = shares_in[last_pair, other, :, 0].reshape(CHIPS * 2 * ROWS, LANES + 128)
            totals[other] += dot(both[:, LANES:], both[:, :LANES], TN)

    def send_second():
        for offset in range(1, PARTS):
            second_copy(offset).start()
        last_in[me] = shares_out[last_pair, me, 1]

    def add_second():
        all_second().wait_recv()
        both = last_in[...].reshape(PARTS * 2 * ROWS, LANES + 128)
        totals[0] += dot(both[:, LANES:], both[:, :LANES], TN)

    forward(0, True, False)

    @pl.when(is_upper)
    def _():
        backward(0, True, False)
        spread_back(1)

    spread_forward(0, False)
    for which in range(2):
        for c in range(CHUNKS):
            turned[which, c] = weights[which, c].T

    def two_ticks(pair, carry):
        tick = 2 * pair + 1
        forward(tick, False, False)
        backward(tick - lag, False, False)
        spread_forward(tick, False)
        spread_back(tick + 1 - lag)

        @pl.when(is_upper)
        def _():
            send_shares(pair)

        forward(tick + 1, False, False)
        backward(tick + 1 - lag, False, False)
        spread_forward(tick + 1, False)
        spread_back(jnp.minimum(tick + 2 - lag, ticks - 2))

        @pl.when(is_lower)
        def _():
            send_shares(pair)

        @pl.when(pair >= 2)
        def _():
            add_shares(pair - 2)

        return carry

    lax.fori_loop(0, ticks // 2 - 1, two_ticks, 0)

    @pl.when(not_last)
    def _():
        copy_copy.wait_recv()

    @pl.when(is_upper)
    def _():
        send_first()

    spread_forward(ticks - 1, True)
    last_hidden = forward(ticks - 1, False, True)

    @pl.when(is_lower)
    def _():
        backward(ticks - 2, False, False)
        send_first()

    backward(ticks - 1, False, True)
    send_second()
    for pair in range(max(last_pair - 2, 0), last_pair):
        add_shares(pair)
    add_first()
    sums_out[...] = totals[1].astype(jnp.bfloat16)
    sums_copy.start()
    give_delta(last_hidden)

    for which in range(2):
        mate_copy(which, 0).wait_send()
        for offset in range(1, CHIPS):
            chip_copy(which, offset).wait_send()
            mate_copy(which, offset).wait_send()

    @pl.when(not_last)
    def _():
        exps_copy.wait_send()

        def drain(tick, carry):
            for c in range(CHUNKS):
                forward_copy(tick, c).wait_send()
            return carry

        lax.fori_loop(1, ticks, drain, 0)

    @pl.when(not_first)
    def _():
        copy_copy.wait_send()

        def drain(tick, carry):
            for c in range(CHUNKS):
                backward_copy(tick, c).wait_send()
            return carry

        lax.fori_loop(1, ticks, drain, 0)

    add_second()
    sums_copy.wait()
    summed = totals[0] + sums_in[...].astype(jnp.float32)
    factor = 1.0 / (ticks * ROWS)
    down_out[...] = (summed[0:RANK] * (own_gain * factor)).astype(jnp.bfloat16)
    up_out[...] = (summed[RANK : 2 * RANK] * factor).astype(jnp.bfloat16)

    def drain_shares(pair, carry):
        all_shares(pair).wait_send()
        return carry

    lax.fori_loop(0, last_pair, drain_shares, 0)
    all_first().wait_send()
    all_second().wait_send()


def per_device(stored_inputs, slot_ids, incoming, delta_exp, grad_exp, norm_gain, down_weight, up_weight):
    stored = stored_inputs[0, 0]
    ticks = delta_exp.shape[2]
    sections = lax.axis_size("section")
    message = (CHUNKS, FOLD * ROWS, LANES)
    bf16, f32 = jnp.bfloat16, jnp.float32
    vmem = pl.BlockSpec(memory_space=pltpu.VMEM)
    operands = (
        slot_ids[0, 0],
        stored,
        incoming[0, 0],
        delta_exp[0, 0],
        grad_exp[0, 0],
        norm_gain,
        down_weight[0].T,
        up_weight[0],
    )
    shares = (ticks // 2, PARTS, 2, 2 * ROWS, LANES + 128)
    down_grad, up_grad, delta = pl.pallas_call(
        functools.partial(kernel, ticks, sections),
        out_shape=(
            jax.ShapeDtypeStruct((RANK, LANES), bf16),
            jax.ShapeDtypeStruct((RANK, LANES), bf16),
            jax.ShapeDtypeStruct(stored.shape[1:], bf16),
        ),
        in_specs=[pl.BlockSpec(memory_space=pl.ANY)] * len(operands),
        out_specs=(vmem, vmem, vmem),
        scratch_shapes=[pltpu.SMEM(operands[0].shape, jnp.int32)]
        + [pltpu.VMEM(operand.shape, operand.dtype) for operand in operands[1:]]
        + [
            pltpu.VMEM((2, CHUNKS, FOLD * RANK, LANES), bf16),
            pltpu.VMEM((2, CHUNKS, LANES, FOLD * RANK), bf16),
            pltpu.VMEM((ticks,) + message, bf16),
            pltpu.VMEM((ticks,) + message, bf16),
            pltpu.VMEM((ticks + 1,) + message, bf16),
            pltpu.VMEM((ticks,) + message, bf16),
            pltpu.VMEM(shares, bf16),
            pltpu.VMEM((ticks // 2, 2, CHIPS, 2, 2 * ROWS, LANES + 128), bf16),
            pltpu.VMEM((PARTS, 2 * ROWS, LANES + 128), bf16),
            pltpu.VMEM(delta_exp.shape[2:], jnp.int32),
            pltpu.VMEM(message, bf16),
            pltpu.VMEM(message, bf16),
            pltpu.VMEM((ticks + 1,) + message, bf16),
            pltpu.VMEM((ticks + 1, ROWS, 128), f32),
            pltpu.VMEM(((ticks + 1) * FOLD * ROWS, FOLD * RANK), f32),
            pltpu.VMEM((ticks + 1, 4, ROWS, 128), f32),
            pltpu.VMEM((2,) + message, f32),
            pltpu.VMEM(message, f32),
            pltpu.VMEM((2, 2 * RANK, LANES), f32),
            pltpu.VMEM((2 * RANK, LANES), bf16),
            pltpu.VMEM((2 * RANK, LANES), bf16),
            pltpu.SemaphoreType.DMA((len(operands),)),
            pltpu.SemaphoreType.DMA((2, 2 * CHIPS)),
            pltpu.SemaphoreType.DMA((2, PARTS)),
            pltpu.SemaphoreType.DMA((ticks, CHUNKS)),
            pltpu.SemaphoreType.DMA((ticks, CHUNKS)),
            pltpu.SemaphoreType.DMA((ticks, CHUNKS)),
            pltpu.SemaphoreType.DMA((ticks, CHUNKS)),
            pltpu.SemaphoreType.DMA((ticks // 2 + 1,)),
            pltpu.SemaphoreType.DMA((ticks // 2 + 1,)),
            pltpu.SemaphoreType.DMA((3,)),
            pltpu.SemaphoreType.DMA((3,)),
        ],
        compiler_params=pltpu.CompilerParams(
            collective_id=0, has_side_effects=True, vmem_limit_bytes=56 * 1024 * 1024
        ),
        name="relay",
    )(*operands)
    return down_grad.T[None], up_grad[None], delta[None, None]


def solution(mesh):
    return jax.shard_map(
        per_device,
        mesh=mesh,
        in_specs=(
            P("section", "dp", None, None, None),
            P("section", "dp", None),
            P("section", "dp", None, None),
            P("section", "dp", None, None, None),
            P("section", "dp", None, None, None),
            P("section", None),
            P("section", "dp", None),
            P("section", None, "dp"),
        ),
        out_specs=(
            P("section", "dp", None),
            P("section", None, "dp"),
            P("section", "dp", None, None),
        ),
        check_vma=False,
    )
```
